32 devices in a mesh: layer: 4 (over x, core), col: 8 (over z, y).
Axes of the slice: x: 2, y: 2, z: 4, core: 2. Of those that a mesh axis runs over, the one named last changes fastest.
Arguments:
- lower_panel: bfloat16 [4, 4096, 768], P('layer', 'col'), may hold values from -0.109375 to 0.109375
- upper_panel: bfloat16 [4, 768, 4096], P('layer', None, 'col'), may hold values from -6 to 6
- diag_inverse: bfloat16 [4, 1, 768, 768], P('layer'), may hold values from -1 to 2, as said below
- pivot_inverse: bfloat16 [2, 128, 128], replicated, may hold values from -0.1 to 0.1, as said below
- pattern: int32 [4, 2, 32], P('layer'), may hold values 0 or 1
- col_order: int32 [32], replicated, may hold values from 0 to 31, each once
- sep_blocks: int32 [2], replicated, may hold values from 0 to 31, as said below
Outputs:
- schur_top: bfloat16 [4096, 4096], P('layer', 'col')
The draws below stay inside these ranges and needn't reach their ends.
Inputs may be any that keep to these rules, and one draw needn't show every extreme that they name: `diag_inverse`: each is the identity plus a full matrix of smaller entries. `pivot_inverse`: full matrices. `sep_blocks`: the 2 entries are distinct.
All inputs are finite; a program needn't handle non-finite values. No bound on the sum of `pattern` on one device may be relied on, other than what follows from the above.
Results may differ from the reference program's by a relative error of at most 0.0088.
Values may be sent and summed in bfloat16 or wider, within the bound.
A program may use at most 64 MiB of HBM per device.

```python
import math
import jax
import jax.numpy as jnp
from jax import lax

S = 4096
SN = 768
NSUP = 1
NB = 128
SEP = 128
LAYERS = 4
LEVELS = 2
NBLK = 32
N_LAYER = 4


def draw_diag_inverse(key, part):
    shape = (LAYERS, NSUP, SN, SN)
    noise = 0.5 * jnp.clip(jax.random.normal(key, shape, jnp.float32), -4.0, 4.0)
    value = jnp.eye(SN, dtype=jnp.float32) + noise / math.sqrt(SN)
    return value.astype(jnp.bfloat16)


def draw_pivot_inverse(key, part):
    shape = (LEVELS, SEP, SEP)
    noise = 0.5 * jnp.clip(jax.random.normal(key, shape, jnp.float32), -4.0, 4.0)
    value = (jnp.eye(SEP, dtype=jnp.float32) + noise / math.sqrt(SEP)) / 32.0
    return value.astype(jnp.bfloat16)


def draw_sep_blocks(key, part):
    order = jax.random.permutation(jax.random.fold_in(key, 17), S // NB)
    return order[:LEVELS].astype(jnp.int32)


def place_ends(array, stream_key, least, top_value):
    spot = [jax.random.randint(jax.random.fold_in(stream_key, axis), (), 0, length) for axis, length in enumerate(array.shape)]
    longest = array.shape.index(max(array.shape))
    neighbour = spot[:longest] + [(spot[longest] + 1) % array.shape[longest]] + spot[longest + 1:]
    return array.at[tuple(spot)].set(least).at[tuple(neighbour)].set(top_value)


def level_of(own_key, shape, split, low, largest):
    factor_of, own = 1.0, jax.random.fold_in(own_key, 6)
    for axis_at, blocks in split:
        draws = jnp.exp(jax.random.uniform(jax.random.fold_in(own, axis_at), (blocks,), jnp.float32, low / len(split), largest / len(split)))
        factor_of = factor_of * jnp.repeat(draws, shape[axis_at] // blocks).reshape([-1 if axis == axis_at else 1 for axis in range(len(shape))])
    return factor_of


def gaussian(stream_key, extent, scale, most, shards=(), held_as=jnp.bfloat16):
    gain = level_of(stream_key, extent, shards, -0.22, 0.18) if shards else 1.0
    entries = jax.random.normal(stream_key, extent, jnp.float32) * scale * gain
    return jnp.minimum(jnp.maximum(entries, -most), most).astype(held_as)


def setup_inputs(seed: int = 0) -> dict:
    keys = jax.random.split(jax.random.key(seed), 8)
    lower_panel = gaussian(keys[0], (LAYERS, S, NSUP * SN), (4 * NSUP * SN) ** -0.5, 0.109375, ((0, 4), (1, 8)))
    upper_panel = gaussian(keys[1], (LAYERS, NSUP * SN, S), 1.0, 6.0, ((0, 4), (2, 8)))
    diag_inverse = draw_diag_inverse(jax.random.fold_in(keys[7], 71), 0)
    pivot_inverse = draw_pivot_inverse(jax.random.fold_in(keys[7], 71), 0)
    pattern = place_ends((jax.random.randint(keys[4], (LAYERS, 2, NBLK), 0, 2) < 1).astype(jnp.int32), jax.random.fold_in(keys[4], 1), 0, 1)
    col_order = jax.random.permutation(keys[5], NBLK).astype(jnp.int32)
    sep_blocks = draw_sep_blocks(jax.random.fold_in(keys[7], 71), 0)
    return {"lower_panel": lower_panel, "upper_panel": upper_panel, "diag_inverse": diag_inverse, "pivot_inverse": pivot_inverse, "pattern": pattern, "col_order": col_order, "sep_blocks": sep_blocks}


def layer_block(lower, upper, inverse, flags):
    width = NSUP * SN
    solved = jnp.einsum("sab,sbc->sac", inverse.astype(jnp.float32), upper.reshape(NSUP, SN, S).astype(jnp.float32))
    right = solved.reshape(width, S).astype(jnp.bfloat16)
    product = jnp.dot(lower, right, preferred_element_type=jnp.float32)
    row_flags = jnp.repeat(flags[0], NB).astype(jnp.float32)
    col_flags = jnp.repeat(flags[1], NB).astype(jnp.float32)
    return (-product * row_flags[:, None] * col_flags[None, :]).astype(jnp.bfloat16)


def eliminate(total, pivot, separator, position):
    panel = lax.dynamic_slice_in_dim(total, (position * NB).astype(jnp.int32), NB, 1).astype(jnp.bfloat16)
    factor = jnp.dot(panel, pivot, preferred_element_type=jnp.float32).astype(jnp.bfloat16)
    upper_rows = lax.dynamic_slice_in_dim(total, (separator * NB).astype(jnp.int32), NB, 0).astype(jnp.bfloat16)
    updated = total - jnp.dot(factor, upper_rows, preferred_element_type=jnp.float32)
    row_keep = (jnp.arange(S, dtype=jnp.int32) // NB) != separator
    col_keep = (jnp.arange(S, dtype=jnp.int32) // NB) != position
    kept = jnp.where(row_keep[:, None] & col_keep[None, :], updated, jnp.zeros_like(updated))
    return kept.astype(jnp.bfloat16)


def reference(lower_panel, upper_panel, diag_inverse, pivot_inverse, pattern, col_order, sep_blocks):
    blocks = []
    for layer_index in range(N_LAYER):
        blocks.append(layer_block(lower_panel[layer_index], upper_panel[layer_index], diag_inverse[layer_index], pattern[layer_index]))
    positions = jnp.arange(NBLK, dtype=jnp.int32)
    for level in range(LEVELS):
        separator = sep_blocks[level].astype(jnp.int32)
        position = jnp.sum(jnp.where(col_order == separator, positions, 0)).astype(jnp.int32)
        joined = []
        for pair_index in range(len(blocks) // 2):
            total = blocks[2 * pair_index].astype(jnp.float32) + blocks[2 * pair_index + 1].astype(jnp.float32)
            joined.append(eliminate(total, pivot_inverse[level], separator, position))
        blocks = joined
    return blocks[0]
```

```python
import functools

import jax
import jax.numpy as jnp
from jax import lax
from jax.experimental import pallas as pl
from jax.experimental.pallas import tpu as pltpu
from jax.sharding import PartitionSpec as P

NB = 128
F32 = jnp.float32
BF16 = jnp.bfloat16
MESH = pl.DeviceIdType.MESH


def dot(a, b):
    return jnp.dot(a, b, preferred_element_type=F32)


def fused_kernel(
    col_count, l_ref, u_ref, d_ref, piv_ref, v0, flag_ref, keep_ref, pat_ref, hot_ref, out_ref,
    lbuf, rbuf, pbuf, cin, xin, vy, vr, vl, vsr, vsl, s_acc, s_own, s_core, s_tot, s_x,
    y_send, yv_send, zr_send, zl_send, vr_send, vl_send, l_recv, vy_recv, vr_recv, vl_recv,
    c_send, c_recv, x_send, x_recv, s_send, s_recv,
):
    piece_rows, width = l_ref.shape
    cols = u_ref.shape[1]
    ext = rbuf.shape[1]
    nz = col_count // 2
    per_piece = piece_rows // NB
    layer = lax.axis_index("layer")
    core, xx = layer % 2, layer // 2
    ci = lax.axis_index("col")
    y, z = ci % 2, ci // 2
    core_peer = {"layer": layer + 1 - 2 * core}
    x_peer = {"layer": layer + 2 - 4 * xx}
    y_peer = {"col": ci + 1 - 2 * y}
    right, left = {"col": ci + 2}, {"col": ci - 2}
    has_right, has_left = z < nz - 1, z > 0

    def copy(src, dst, send, recv, peer):
        return pltpu.make_async_remote_copy(
            src_ref=src, dst_ref=dst, send_sem=send, recv_sem=recv, device_id=peer, device_id_type=MESH
        )

    def piece(p):
        return pl.ds(pl.multiple_of(p * piece_rows, piece_rows), piece_rows)

    barrier = pltpu.get_barrier_semaphore()
    for peer in (core_peer, x_peer, y_peer):
        pl.semaphore_signal(barrier, inc=1, device_id=peer, device_id_type=MESH)

    @pl.when(has_right)
    def _():
        pl.semaphore_signal(barrier, inc=1, device_id=right, device_id_type=MESH)

    @pl.when(has_left)
    def _():
        pl.semaphore_signal(barrier, inc=1, device_id=left, device_id_type=MESH)

    pl.semaphore_wait(barrier, 3 + jnp.where(has_right, 1, 0) + jnp.where(has_left, 1, 0))

    parts = v0.shape[0] // (2 * NB)

    def vpart(k):
        return pl.ds(k * 2 * NB, 2 * NB)

    def v_y(k):
        return copy(v0.at[vpart(k)], vy.at[vpart(k)], yv_send.at[k], vy_recv.at[k], y_peer)

    def v_right(k):
        return copy(vsr.at[vpart(k)], vr.at[vpart(k)], vr_send.at[k], vr_recv.at[k], right)

    def v_left(k):
        return copy(vsl.at[vpart(k)], vl.at[vpart(k)], vl_send.at[k], vl_recv.at[k], left)

    for k in range(parts):
        v_y(k).start()

    lbuf[piece(ci), :] = l_ref[...]

    def z_right(p):
        return copy(lbuf.at[piece(p)], lbuf.at[piece(p)], zr_send.at[p // 2], l_recv.at[p], right)

    def z_left(p):
        return copy(lbuf.at[piece(p)], lbuf.at[piece(p)], zl_send.at[p // 2], l_recv.at[p], left)

    def over_y(p):
        return copy(lbuf.at[piece(p)], lbuf.at[piece(p)], y_send.at[p // 2], l_recv.at[p], y_peer)

    @pl.when(has_right)
    def _():
        z_right(ci).start()

    @pl.when(has_left)
    def _():
        z_left(ci).start()

    over_y(ci).start()

    supers, node = d_ref.shape[0], d_ref.shape[1]
    for s in range(supers):
        solved = dot(d_ref[s], u_ref[s * node : (s + 1) * node, :])
        rounded = solved.astype(BF16).astype(F32)
        rbuf[s * node : (s + 1) * node, 0:cols] = (rounded * flag_ref[:, 0:cols]).astype(BF16)

    for k in range(parts):
        rows = vpart(k)
        v_y(k).wait_recv()
        v0_sum = v0[rows, :] + vy[rows, :]
        vsr[rows, :] = v0_sum
        vsl[rows, :] = v0_sum

        def go_right(k=k, rows=rows):
            @pl.when(has_left)
            def _():
                v_right(k).wait_recv()
                vsr[rows, :] = vsr[rows, :] + vr[rows, :]

            @pl.when(has_right)
            def _():
                v_right(k).start()

        def go_left(k=k, rows=rows):
            @pl.when(has_right)
            def _():
                v_left(k).wait_recv()
                vsl[rows, :] = vsl[rows, :] + vl[rows, :]

            @pl.when(has_left)
            def _():
                v_left(k).start()

        pl.when(z < nz // 2)(go_right)
        pl.when(z >= nz // 2)(go_left)

    for k in range(parts):
        rows = vpart(k)

        def go_right(k=k, rows=rows):
            v_right(k).wait_recv()
            vsr[rows, :] = vsr[rows, :] + vr[rows, :]

            @pl.when(has_right)
            def _():
                v_right(k).start()

        def go_left(k=k, rows=rows):
            v_left(k).wait_recv()
            vsl[rows, :] = vsl[rows, :] + vl[rows, :]

            @pl.when(has_left)
            def _():
                v_left(k).start()

        pl.when(z < nz // 2)(go_left)
        pl.when(z >= nz // 2)(go_right)

    vall = vsr[...] + vsl[...] - (v0[...] + vy[...])
    for s in range(supers):
        solved = dot(d_ref[s], vall[s * node : (s + 1) * node, :])
        rounded = solved.astype(BF16).astype(F32)
        rbuf[s * node : (s + 1) * node, cols:ext] = (rounded * flag_ref[:, cols:ext]).astype(BF16)

    s_acc[...] = jnp.zeros_like(s_acc)
    per_span = col_count // 4

    def slot_of(p):
        return (p // per_span // 2) * per_span + p % per_span

    def to_core(p):
        return copy(pbuf.at[piece(p)], cin.at[slot_of(p)], c_send.at[slot_of(p)], c_recv.at[slot_of(p)], core_peer)

    def to_x(p):
        return copy(pbuf.at[piece(p)], xin.at[p % per_span], x_send.at[p % per_span], x_recv.at[p % per_span], x_peer)

    def process(p):
        rows = lbuf[piece(p), :]
        for n in range(0, ext, 2 * NB):
            acc = dot(rows, rbuf[:, n : n + 2 * NB])
            found = [None, None]
            for j in range(per_piece):
                block = p * per_piece + j
                flagged = acc[j * NB : (j + 1) * NB] * pat_ref[0, block].astype(F32)
                pbuf[pl.ds(pl.multiple_of(block * NB, NB), NB), n : n + 2 * NB] = flagged.astype(BF16)
                for k in range(2):
                    term = flagged * hot_ref[k, block]
                    found[k] = term if j == 0 else found[k] + term
            for k in range(2):
                s_acc[k * NB : (k + 1) * NB, n : n + 2 * NB] += found[k]
        span = p // per_span

        @pl.when(span % 2 != core)
        def _():
            to_core(p).start()

        @pl.when(span % 2 == core)
        def _():
            to_core(p).wait_recv()
            slot = slot_of(p)

            @pl.loop(0, per_piece)
            def _(j):
                at = pl.ds(pl.multiple_of(p * piece_rows + j * NB, NB), NB)
                here = pl.ds(pl.multiple_of(j * NB, NB), NB)
                pbuf[at, :] = (pbuf[at, :].astype(F32) + cin[slot, here, :].astype(F32)).astype(BF16)

            @pl.when(span // 2 != xx)
            def _():
                to_x(p).start()

    def place(i):
        dist = (i + 1) // 2
        return z + dist * (1 - 2 * (i % 2))

    events = 2 * nz - 1

    @pl.loop(0, events + 2)
    def _(i):
        zc = place(i)

        @pl.when((i < events) & (zc >= 0) & (zc < nz))
        def _():
            p = zc * 2 + y

            @pl.when(i > 0)
            def _():
                over_y(p).wait_recv()

                @pl.when(has_right & (zc < z))
                def _():
                    z_right(p).start()

                @pl.when(has_left & (zc > z))
                def _():
                    z_left(p).start()

                over_y(p).start()

            process(p)

        zo = place(jnp.maximum(i - 2, 0))

        @pl.when((i >= 2) & (zo >= 0) & (zo < nz))
        def _():
            p = zo * 2 + 1 - y
            over_y(p).wait_recv()
            process(p)

    def s_copy(src, dst, k, peer):
        return copy(src, dst, s_send.at[k], s_recv.at[k], peer)

    s_own[...] = s_acc[...].astype(BF16)
    swap = s_copy(s_own, s_core, 0, core_peer)
    swap.start()
    swap.wait()
    s_tot[...] = (s_own[...].astype(F32) + s_core[...].astype(F32)).astype(BF16)
    mine = pl.ds(pl.multiple_of(core * NB, NB), NB)
    over_x = s_copy(s_tot.at[mine], s_x.at[mine], 1, x_peer)
    over_x.start()
    over_x.wait_recv()
    share = s_copy(s_x.at[mine], s_x.at[mine], 2, core_peer)
    share.start()
    share.wait_recv()

    pos_col = [cols, cols + NB]
    upper = jnp.concatenate([s_tot[0:NB, 0:cols], s_x[0:NB, 0:cols]], axis=0)
    upper_p = jnp.concatenate([s_tot[0:NB, pos_col[1] : ext], s_x[0:NB, pos_col[1] : ext]], axis=0)
    keep_c = [keep_ref[k : k + 1, :] for k in range(2)]

    def factors(a, b):
        return jnp.concatenate([dot(a, piv_ref[0]).astype(BF16), dot(b, piv_ref[0]).astype(BF16)], axis=1)

    fs = factors(s_tot[NB : 2 * NB, cols : cols + NB], s_x[NB : 2 * NB, cols : cols + NB])
    last = s_tot[NB : 2 * NB, 0:cols].astype(F32) + s_x[NB : 2 * NB, 0:cols].astype(F32)
    upper2 = ((last - dot(fs, upper)) * keep_c[0]).astype(BF16)

    for q in range(per_span):
        p = layer * per_span + q

        to_x(p).wait_recv()
        at = piece(p)
        f0 = factors(pbuf[at, cols : cols + NB], xin[q, :, cols : cols + NB])

        def keep_rows(value, k):
            kept = [
                value[j * NB : (j + 1) * NB] * (1.0 - hot_ref[k, p * per_piece + j]) for j in range(per_piece)
            ]
            return jnp.concatenate(kept, axis=0)

        panel = pbuf[at, pos_col[1] : ext].astype(F32) + xin[q, :, pos_col[1] : ext].astype(F32)
        panel = keep_rows(panel - dot(f0, upper_p), 0).astype(BF16)
        f2 = dot(panel, piv_ref[1]).astype(BF16)
        total = pbuf[at, 0:cols].astype(F32) + xin[q, :, 0:cols].astype(F32)
        total = keep_rows(total - dot(f0, upper), 0) * keep_c[0]
        final = keep_rows(total - dot(f2, upper2), 1) * keep_c[1]
        out_ref[q * piece_rows : (q + 1) * piece_rows, :] = final.astype(BF16)

    over_x.wait_send()
    share.wait_send()
    for k in range(parts):
        v_y(k).wait_send()

        @pl.when(has_right)
        def _():
            v_right(k).wait_send()

        @pl.when(has_left)
        def _():
            v_left(k).wait_send()

    @pl.loop(0, nz)
    def _(zc):
        p = zc * 2 + y
        over_y(p).wait_send()

        @pl.when(has_right & (zc <= z))
        def _():
            z_right(p).wait_send()

        @pl.when(has_left & (zc >= z))
        def _():
            z_left(p).wait_send()

    @pl.loop(0, col_count)
    def _(p):
        span = p // per_span

        @pl.when(span % 2 != core)
        def _():
            to_core(p).wait_send()

        @pl.when((span % 2 == core) & (span // 2 != xx))
        def _():
            to_x(p).wait_send()


def fused(lower_panel, upper_panel, diag_inverse, pivot_inverse, pattern, col_order, sep_blocks):
    col_count = lax.axis_size("col")
    piece_rows, width = lower_panel.shape[1:]
    cols = upper_panel.shape[2]
    ext = cols + 2 * NB
    nz, slots = col_count // 2, col_count // 2
    total_rows = piece_rows * col_count
    per_span = col_count // 4
    parts = width // (2 * NB)
    positions = jnp.arange(col_order.shape[0], dtype=jnp.int32)
    pos = jnp.sum(jnp.where(col_order[None, :] == sep_blocks[:, None], positions[None, :], 0), axis=1)
    blocks = cols // NB
    first = lax.axis_index("col") * blocks
    masked = []
    for k in range(2):
        local = pos[k] - first
        inside = (local >= 0) & (local < blocks)
        taken = lax.dynamic_slice_in_dim(upper_panel[0], jnp.clip(local, 0, blocks - 1) * NB, NB, 1)
        masked.append(jnp.where(inside, taken, jnp.zeros_like(taken)))
    masked = jnp.concatenate(masked, axis=1)
    own_flags = lax.dynamic_slice_in_dim(pattern[0, 1], first, blocks)
    flags = -jnp.repeat(jnp.concatenate([own_flags, pattern[0, 1][pos]]), NB)[None, :].astype(F32)
    col_block = first + jnp.arange(cols, dtype=jnp.int32) // NB
    keep = (col_block[None, :] != pos[:, None]).astype(F32)
    hot = (positions[None, :] == sep_blocks[:, None]).astype(F32)
    vmem = pl.BlockSpec(memory_space=pltpu.VMEM)
    smem = pl.BlockSpec(memory_space=pltpu.SMEM)
    dma = pltpu.SemaphoreType.DMA
    v_shape = pltpu.VMEM((width, 2 * NB), BF16)
    s_shape = pltpu.VMEM((2 * NB, ext), BF16)
    return pl.pallas_call(
        functools.partial(fused_kernel, col_count),
        out_shape=jax.ShapeDtypeStruct((per_span * piece_rows, cols), BF16),
        in_specs=[vmem] * 7 + [smem] * 2,
        out_specs=vmem,
        scratch_shapes=[
            pltpu.VMEM((total_rows, width), BF16),
            pltpu.VMEM((width, ext), BF16),
            pltpu.VMEM((total_rows, ext), BF16),
            pltpu.VMEM((slots, piece_rows, ext), BF16),
            pltpu.VMEM((per_span, piece_rows, ext), BF16),
            v_shape, v_shape, v_shape, v_shape, v_shape,
            pltpu.VMEM((2 * NB, ext), F32), s_shape, s_shape, s_shape, s_shape,
            dma((nz,)), dma((parts,)), dma((nz,)), dma((nz,)), dma((parts,)), dma((parts,)),
            dma((col_count,)), dma((parts,)), dma((parts,)), dma((parts,)),
            dma((slots,)), dma((slots,)), dma((per_span,)), dma((per_span,)), dma((3,)), dma((3,)),
        ],
        compiler_params=pltpu.CompilerParams(
            collective_id=0, has_side_effects=True, vmem_limit_bytes=56 * 2**20
        ),
        cost_estimate=pl.CostEstimate(flops=6 * 10**9, bytes_accessed=5 * 10**6, transcendentals=0),
    )(
        lower_panel[0], upper_panel[0], diag_inverse[0], pivot_inverse, masked, flags, keep,
        pattern[0], hot,
    )


def from_partner(value, axis, distance):
    mask = 2**distance
    pairs = [(source, source ^ mask) for source in range(lax.axis_size(axis))]
    return lax.ppermute(value, axis, pairs)


def broadcast(x, axis, root):
    mine = lax.axis_index(axis) == root
    return lax.psum(jnp.where(mine, x, jnp.zeros_like(x)), axis)


def share_rows(values, level):
    for bit in range(level + 1):
        other = from_partner(values, "layer", bit)
        values = (values.astype(jnp.float32) + other.astype(jnp.float32)).astype(jnp.bfloat16)
    return values


def shards(lower_panel, upper_panel, diag_inverse, pivot_inverse, pattern, col_order, sep_blocks):
    supernodes = diag_inverse.shape[1]
    node_width = diag_inverse.shape[2]
    local_cols = upper_panel.shape[2]
    col_index = lax.axis_index("col")
    first_col = col_index * local_cols
    nblocks = col_order.shape[0]
    solved = jnp.einsum(
        "sab,sbc->sac",
        diag_inverse[0],
        upper_panel[0].reshape(supernodes, node_width, local_cols),
        preferred_element_type=jnp.float32,
    )
    right = solved.astype(jnp.bfloat16).reshape(supernodes * node_width, local_cols)
    row_flags = jnp.repeat(pattern[0, 0], NB).astype(jnp.float32)
    all_col_flags = jnp.repeat(pattern[0, 1], NB).astype(jnp.float32)
    col_flags = lax.dynamic_slice_in_dim(all_col_flags, first_col, local_cols)
    product = jnp.dot(
        lax.all_gather(lower_panel[0], "col", axis=0, tiled=True),
        right,
        preferred_element_type=jnp.float32,
    )
    current = (-product * row_flags[:, None] * col_flags[None, :]).astype(jnp.bfloat16)
    layer_count = lax.axis_size("layer")
    layer_index = lax.axis_index("layer")
    levels = layer_count.bit_length() - 1
    positions = jnp.arange(nblocks, dtype=jnp.int32)
    total_rows = current.shape[0]
    span_rows = total_rows // layer_count
    col_blocks = (first_col + jnp.arange(local_cols, dtype=jnp.int32)) // NB
    held = current.reshape(layer_count, span_rows, local_cols)
    for level in range(levels):
        count = held.shape[0] // 2
        paired = held.reshape(count, 2, span_rows, local_cols)
        side = layer_index >> level & 1
        keep_half = lax.dynamic_index_in_dim(paired, side, 1, keepdims=False)
        send_half = lax.dynamic_index_in_dim(paired, 1 - side, 1, keepdims=False)
        partner = from_partner(send_half, "layer", level)
        total = keep_half.astype(jnp.float32) + partner.astype(jnp.float32)
        stride = 2 ** (level + 1)
        base = layer_index % stride
        span_ids = base + stride * jnp.arange(count, dtype=jnp.int32)
        global_rows = (
            span_ids[:, None] * span_rows + jnp.arange(span_rows, dtype=jnp.int32)[None, :]
        ).reshape(count * span_rows)
        separator = sep_blocks[level]
        position = jnp.sum(jnp.where(col_order == separator, positions, 0))
        owner = position * NB // local_cols
        offset = position * NB - owner * local_cols
        sep_row = separator * NB
        sep_span = sep_row // span_rows
        inner = sep_row - sep_span * span_rows
        holds = sep_span % stride == base
        local_span = jnp.where(holds, sep_span // stride, 0)
        zero = jnp.zeros((), jnp.int32)
        rows_here = lax.dynamic_slice(
            total, (local_span, inner, zero), (1, NB, local_cols)
        ).reshape(NB, local_cols)
        masked = jnp.where(holds, rows_here, jnp.zeros_like(rows_here)).astype(jnp.bfloat16)
        upper_rows = share_rows(masked, level)
        flat = total.reshape(count * span_rows, local_cols)
        local_panel = lax.dynamic_slice_in_dim(flat, offset, NB, 1).astype(jnp.bfloat16)
        local_factor = jnp.dot(
            local_panel, pivot_inverse[level], preferred_element_type=jnp.float32
        ).astype(jnp.bfloat16)
        factor = broadcast(local_factor, "col", owner)
        updated = flat - jnp.dot(factor, upper_rows, preferred_element_type=jnp.float32)
        keep = (global_rows // NB != separator)[:, None] & (col_blocks != position)[None, :]
        kept = jnp.where(keep, updated, jnp.zeros_like(updated)).astype(jnp.bfloat16)
        held = kept.reshape(count, span_rows, local_cols)
    result = held.reshape(span_rows, local_cols)
    return result


def fits(mesh, args):
    layers, columns = mesh.shape["layer"], mesh.shape["col"]
    lower_panel, upper_panel, diag_inverse = args[:3]
    rows, width = lower_panel.shape[1] // columns, lower_panel.shape[2]
    cols = upper_panel.shape[2] // columns
    return (
        layers == 4
        and columns % layers == 0
        and rows % NB == 0
        and cols % (2 * NB) == 0
        and width % (2 * NB) == 0
        and diag_inverse.shape[2] % NB == 0
    )


def solution(mesh):
    in_specs = (
        P("layer", "col", None),
        P("layer", None, "col"),
        P("layer", None, None, None),
        P(),
        P("layer", None, None),
        P(),
        P(),
    )
    out_specs = P("layer", "col")

    def run(*args):
        body = fused if fits(mesh, args) else shards
        return jax.shard_map(body, mesh=mesh, in_specs=in_specs, out_specs=out_specs, check_vma=False)(*args)

    return run
```

```python
import functools

import jax
import jax.numpy as jnp
from jax import lax
from jax.experimental import pallas as pl
from jax.experimental.pallas import tpu as pltpu
from jax.sharding import PartitionSpec as P

NB = 128
F32 = jnp.float32
BF16 = jnp.bfloat16
MESH = pl.DeviceIdType.MESH


def dot(a, b):
    return jnp.dot(a, b, preferred_element_type=F32)


def fused_kernel(
    col_count, l_ref, u_ref, d_ref, piv_ref, pat_ref, ord_ref, sep_ref, out_ref,
    lbuf, rbuf, pbuf, cin, xin, v0, vbase, vy, vr, vl, vsr, vsl, s_acc, s_own, s_core, s_tot, s_x,
    y_send, yb_send, yv_send, zr_send, zl_send, br_send, bl_send, vr_send, vl_send, l_recv, b_recv, vy_recv, vr_recv, vl_recv,
    c_send, c_recv, x_send, x_recv, s_send, s_recv,
):
    piece_rows, width = l_ref.shape
    cols = u_ref.shape[1]
    ext = rbuf.shape[1]
    nz = col_count // 2
    blocks = cols // NB
    per_piece = piece_rows // NB
    few = max(piece_rows // 8, 16)
    layer = lax.axis_index("layer")
    core, xx = layer % 2, layer // 2
    ci = lax.axis_index("col")
    y, z = ci % 2, ci // 2
    core_peer = {"layer": layer + 1 - 2 * core}
    x_peer = {"layer": layer + 2 - 4 * xx}
    y_peer = {"col": ci + 1 - 2 * y}
    right, left = {"col": ci + 2}, {"col": ci - 2}
    has_right, has_left = z < nz - 1, z > 0
    first = ci * blocks

    def one_if(condition):
        return jnp.where(condition, 1.0, 0.0).astype(F32)

    def hot_row(k, block):
        return one_if(sep_ref[k] == block)

    def hot_col(k, b):
        return one_if(ord_ref[first + b] == sep_ref[k])


    def copy(src, dst, send, recv, peer):
        return pltpu.make_async_remote_copy(
            src_ref=src, dst_ref=dst, send_sem=send, recv_sem=recv, device_id=peer, device_id_type=MESH
        )

    def piece(p):
        return pl.ds(pl.multiple_of(p * piece_rows, piece_rows), piece_rows)

    barrier = pltpu.get_barrier_semaphore()
    for peer in (core_peer, x_peer, y_peer):
        pl.semaphore_signal(barrier, inc=1, device_id=peer, device_id_type=MESH)

    @pl.when(has_right)
    def _():
        pl.semaphore_signal(barrier, inc=1, device_id=right, device_id_type=MESH)

    @pl.when(has_left)
    def _():
        pl.semaphore_signal(barrier, inc=1, device_id=left, device_id_type=MESH)

    for k in range(2):
        taken = u_ref[:, 0:NB].astype(F32) * hot_col(k, 0)
        for b in range(1, blocks):
            taken = taken + u_ref[:, b * NB : (b + 1) * NB].astype(F32) * hot_col(k, b)
        v0[:, k * NB : (k + 1) * NB] = taken.astype(BF16)

    pl.semaphore_wait(barrier, 3 + jnp.where(has_right, 1, 0) + jnp.where(has_left, 1, 0))

    parts = 4
    part = v0.shape[0] // parts
    y_first, z_first = (0, 1), (2, 3)

    def vpart(k):
        return pl.ds(k * part, part)

    def v_y(k):
        src = v0 if k in y_first else vbase
        return copy(src.at[vpart(k)], vy.at[vpart(k)], yv_send.at[k], vy_recv.at[k], y_peer)

    def v_right(k):
        return copy(vsr.at[vpart(k)], vr.at[vpart(k)], vr_send.at[k], vr_recv.at[k], right)

    def v_left(k):
        return copy(vsl.at[vpart(k)], vl.at[vpart(k)], vl_send.at[k], vl_recv.at[k], left)

    def add_right(k):
        rows = vpart(k)

        @pl.when(has_left)
        def _():
            v_right(k).wait_recv()
            vsr[rows, :] = vsr[rows, :] + vr[rows, :]

        @pl.when(has_right)
        def _():
            v_right(k).start()

    def add_left(k):
        rows = vpart(k)

        @pl.when(has_right)
        def _():
            v_left(k).wait_recv()
            vsl[rows, :] = vsl[rows, :] + vl[rows, :]

        @pl.when(has_left)
        def _():
            v_left(k).start()

    def near_way(k):
        pl.when(z < nz // 2)(functools.partial(add_right, k))
        pl.when(z >= nz // 2)(functools.partial(add_left, k))

    def far_way(k):
        pl.when(z < nz // 2)(functools.partial(add_left, k))
        pl.when(z >= nz // 2)(functools.partial(add_right, k))

    for k in y_first:
        v_y(k).start()
    vsr[...] = v0[...]
    vsl[...] = v0[...]

    @pl.when(z == 0)
    def _():
        for k in z_first:
            v_right(k).start()

    @pl.when(z == nz - 1)
    def _():
        for k in z_first:
            v_left(k).start()

    lbuf[piece(ci), :] = l_ref[...]

    def head(p):
        return pl.ds(pl.multiple_of(p * piece_rows, piece_rows), piece_rows - few)

    def tail(p):
        return pl.ds(pl.multiple_of(p * piece_rows + (piece_rows - few), few), few)

    def z_right(p):
        return copy(lbuf.at[piece(p)], lbuf.at[piece(p)], zr_send.at[p // 2], l_recv.at[p], right)

    def z_left(p):
        return copy(lbuf.at[piece(p)], lbuf.at[piece(p)], zl_send.at[p // 2], l_recv.at[p], left)

    def tail_right(p):
        return copy(lbuf.at[tail(p)], lbuf.at[tail(p)], br_send.at[p // 2], b_recv.at[p], right)

    def tail_left(p):
        return copy(lbuf.at[tail(p)], lbuf.at[tail(p)], bl_send.at[p // 2], b_recv.at[p], left)

    def over_y(p):
        return copy(lbuf.at[head(p)], lbuf.at[head(p)], y_send.at[p // 2], l_recv.at[p], y_peer)

    def tail_over_y(p):
        return copy(lbuf.at[tail(p)], lbuf.at[tail(p)], yb_send.at[0], b_recv.at[p], y_peer)

    tail_over_y(ci).start()

    @pl.when(has_right)
    def _():
        z_right(ci).start()

    @pl.when(has_left)
    def _():
        z_left(ci).start()

    over_y(ci).start()

    supers, node = d_ref.shape[0], d_ref.shape[1]
    for s in range(supers):
        solved = dot(d_ref[s], u_ref[s * node : (s + 1) * node, :])
        rounded = solved.astype(BF16).astype(F32)
        for b in range(blocks):
            flag = -pat_ref[1, first + b].astype(F32)
            rbuf[s * node : (s + 1) * node, b * NB : (b + 1) * NB] = (
                rounded[:, b * NB : (b + 1) * NB] * flag
            ).astype(BF16)

    s_acc[...] = jnp.zeros_like(s_acc)

    @pl.when((z > 0) & (z < nz - 1))
    def _():
        for k in z_first:
            near_way(k)

    for k in y_first:
        rows = vpart(k)
        v_y(k).wait_recv()
        summed = v0[rows, :] + vy[rows, :]
        vbase[rows, :] = summed
        vsr[rows, :] = summed
        vsl[rows, :] = summed
        near_way(k)
    for k in z_first:
        rows = vpart(k)
        far_way(k)
        vbase[rows, :] = vsr[rows, :] + vsl[rows, :] - v0[rows, :]
        v_y(k).start()
    for k in y_first:
        far_way(k)

    other = ci + 1 - 2 * y
    tail_over_y(other).wait_recv()

    @pl.when(has_right)
    def _():
        tail_right(other).start()

    @pl.when(has_left)
    def _():
        tail_left(other).start()

    for k in z_first:
        rows = vpart(k)
        v_y(k).wait_recv()
        v0[rows, :] = vbase[rows, :] + vy[rows, :]
    for k in y_first:
        rows = vpart(k)
        v_y(k).wait_send()
        v0[rows, :] = vsr[rows, :] + vsl[rows, :] - vbase[rows, :]
    for s in range(supers):
        solved = dot(d_ref[s], v0[s * node : (s + 1) * node, :])
        rounded = solved.astype(BF16).astype(F32)
        for k in range(2):
            held = jnp.int32(0)
            for p in range(ord_ref.shape[0]):
                held = held + jnp.where(ord_ref[p] == sep_ref[k], pat_ref[1, p], 0)
            rbuf[s * node : (s + 1) * node, cols + k * NB : cols + (k + 1) * NB] = (
                rounded[:, k * NB : (k + 1) * NB] * -held.astype(F32)
            ).astype(BF16)

    per_span = col_count // 4

    def slot_of(p):
        return (p // per_span // 2) * per_span + p % per_span

    def to_core(p):
        return copy(pbuf.at[piece(p)], cin.at[slot_of(p)], c_send.at[slot_of(p)], c_recv.at[slot_of(p)], core_peer)

    def to_x(p):
        return copy(pbuf.at[piece(p)], xin.at[p % per_span], x_send.at[p % per_span], x_recv.at[p % per_span], x_peer)

    def process(p):
        rows = lbuf[piece(p), :]
        for n in range(0, ext, 2 * NB):
            acc = dot(rows, rbuf[:, n : n + 2 * NB])
            found = [None, None]
            for j in range(per_piece):
                block = p * per_piece + j
                flagged = acc[j * NB : (j + 1) * NB] * pat_ref[0, block].astype(F32)
                pbuf[pl.ds(pl.multiple_of(block * NB, NB), NB), n : n + 2 * NB] = flagged.astype(BF16)
                for k in range(2):
                    term = flagged * hot_row(k, block)
                    found[k] = term if j == 0 else found[k] + term
            for k in range(2):
                s_acc[k * NB : (k + 1) * NB, n : n + 2 * NB] += found[k]
        span = p // per_span

        @pl.when(span % 2 != core)
        def _():
            to_core(p).start()

    def finish(p):
        span = p // per_span

        @pl.when(span % 2 == core)
        def _():
            to_core(p).wait_recv()
            slot = slot_of(p)

            @pl.loop(0, per_piece)
            def _(j):
                at = pl.ds(pl.multiple_of(p * piece_rows + j * NB, NB), NB)
                here = pl.ds(pl.multiple_of(j * NB, NB), NB)
                pbuf[at, :] = (pbuf[at, :].astype(F32) + cin[slot, here, :].astype(F32)).astype(BF16)

            @pl.when(span // 2 != xx)
            def _():
                to_x(p).start()

    @pl.loop(0, nz)
    def _(step):
        for way in (1, -1):
            zc = z + way * (step + 1)

            @pl.when((zc >= 0) & (zc < nz))
            def _(zc=zc, way=way):
                p, o = zc * 2 + y, zc * 2 + 1 - y
                z_right(p).wait_recv()
                on = has_left if way > 0 else has_right

                @pl.when(on)
                def _():
                    (z_left if way > 0 else z_right)(p).start()

                over_y(p).start()
                tail_right(o).wait_recv()

                @pl.when(on)
                def _():
                    (tail_left if way > 0 else tail_right)(o).start()

        def candidate(t):
            zc = z + step * (1 - 2 * (t % 2))
            line = jnp.where(t < 2, y, 1 - y)
            valid = (zc >= 0) & (zc < nz) & ((step > 0) | (t % 2 == 0))
            return zc * 2 + line, valid

        @pl.loop(0, 5)
        def _(t):
            p, valid = candidate(t)

            @pl.when((t < 4) & valid)
            def _():
                @pl.when(t >= 2)
                def _():
                    over_y(p).wait_recv()

                process(p)

            before, valid_before = candidate(jnp.maximum(t - 1, 0))

            @pl.when((t > 0) & valid_before)
            def _():
                finish(before)

    def s_copy(src, dst, k, peer):
        return copy(src, dst, s_send.at[k], s_recv.at[k], peer)

    s_own[...] = s_acc[...].astype(BF16)
    swap = s_copy(s_own, s_core, 0, core_peer)
    swap.start()
    swap.wait()
    s_tot[...] = (s_own[...].astype(F32) + s_core[...].astype(F32)).astype(BF16)
    mine = pl.ds(pl.multiple_of(core * NB, NB), NB)
    over_x = s_copy(s_tot.at[mine], s_x.at[mine], 1, x_peer)
    over_x.start()
    over_x.wait_recv()
    share = s_copy(s_x.at[mine], s_x.at[mine], 2, core_peer)
    share.start()
    share.wait_recv()

    pos_col = [cols, cols + NB]
    upper = jnp.concatenate([s_tot[0:NB, 0:cols], s_x[0:NB, 0:cols]], axis=0)
    upper_p = jnp.concatenate([s_tot[0:NB, pos_col[1] : ext], s_x[0:NB, pos_col[1] : ext]], axis=0)
    keep_c = [
        jnp.concatenate([jnp.full((1, NB), 1.0, F32) * (1.0 - hot_col(k, b)) for b in range(blocks)], axis=1)
        for k in range(2)
    ]

    def factors(a, b):
        return jnp.concatenate([dot(a, piv_ref[0]).astype(BF16), dot(b, piv_ref[0]).astype(BF16)], axis=1)

    fs = factors(s_tot[NB : 2 * NB, cols : cols + NB], s_x[NB : 2 * NB, cols : cols + NB])
    last = s_tot[NB : 2 * NB, 0:cols].astype(F32) + s_x[NB : 2 * NB, 0:cols].astype(F32)
    upper2 = ((last - dot(fs, upper)) * keep_c[0]).astype(BF16)

    for q in range(per_span):
        p = layer * per_span + q

        to_x(p).wait_recv()
        at = piece(p)
        f0 = factors(pbuf[at, cols : cols + NB], xin[q, :, cols : cols + NB])

        def keep_rows(value, k):
            kept = [
                value[j * NB : (j + 1) * NB] * (1.0 - hot_row(k, p * per_piece + j)) for j in range(per_piece)
            ]
            return jnp.concatenate(kept, axis=0)

        panel = pbuf[at, pos_col[1] : ext].astype(F32) + xin[q, :, pos_col[1] : ext].astype(F32)
        panel = keep_rows(panel - dot(f0, upper_p), 0).astype(BF16)
        f2 = dot(panel, piv_ref[1]).astype(BF16)
        total = pbuf[at, 0:cols].astype(F32) + xin[q, :, 0:cols].astype(F32)
        total = keep_rows(total - dot(f0, upper), 0) * keep_c[0]
        final = keep_rows(total - dot(f2, upper2), 1) * keep_c[1]
        out_ref[q * piece_rows : (q + 1) * piece_rows, :] = final.astype(BF16)

    over_x.wait_send()
    share.wait_send()
    for k in range(parts):
        if k in z_first:
            v_y(k).wait_send()

        @pl.when(has_right)
        def _():
            v_right(k).wait_send()

        @pl.when(has_left)
        def _():
            v_left(k).wait_send()

    tail_over_y(ci).wait_send()

    @pl.loop(0, nz)
    def _(zc):
        p, o = zc * 2 + y, zc * 2 + 1 - y
        over_y(p).wait_send()

        @pl.when(has_right & (zc <= z))
        def _():
            z_right(p).wait_send()
            tail_right(o).wait_send()

        @pl.when(has_left & (zc >= z))
        def _():
            z_left(p).wait_send()
            tail_left(o).wait_send()

    @pl.loop(0, col_count)
    def _(p):
        span = p // per_span

        @pl.when(span % 2 != core)
        def _():
            to_core(p).wait_send()

        @pl.when((span % 2 == core) & (span // 2 != xx))
        def _():
            to_x(p).wait_send()


def fused(lower_panel, upper_panel, diag_inverse, pivot_inverse, pattern, col_order, sep_blocks):
    col_count = lax.axis_size("col")
    piece_rows, width = lower_panel.shape[1:]
    cols = upper_panel.shape[2]
    ext = cols + 2 * NB
    nz, slots = col_count // 2, col_count // 2
    total_rows = piece_rows * col_count
    per_span = col_count // 4
    parts = 4
    vmem = pl.BlockSpec(memory_space=pltpu.VMEM)
    smem = pl.BlockSpec(memory_space=pltpu.SMEM)
    dma = pltpu.SemaphoreType.DMA
    v_shape = pltpu.VMEM((width, 2 * NB), BF16)
    s_shape = pltpu.VMEM((2 * NB, ext), BF16)
    return pl.pallas_call(
        functools.partial(fused_kernel, col_count),
        out_shape=jax.ShapeDtypeStruct((per_span * piece_rows, cols), BF16),
        in_specs=[vmem] * 4 + [smem] * 3,
        out_specs=vmem,
        scratch_shapes=[
            pltpu.VMEM((total_rows, width), BF16),
            pltpu.VMEM((width, ext), BF16),
            pltpu.VMEM((total_rows, ext), BF16),
            pltpu.VMEM((slots, piece_rows, ext), BF16),
            pltpu.VMEM((per_span, piece_rows, ext), BF16),
            v_shape, v_shape, v_shape, v_shape, v_shape, v_shape, v_shape,
            pltpu.VMEM((2 * NB, ext), F32), s_shape, s_shape, s_shape, s_shape,
            dma((nz,)), dma((1,)), dma((parts,)), dma((nz,)), dma((nz,)), dma((nz,)), dma((nz,)), dma((parts,)), dma((parts,)),
            dma((col_count,)), dma((col_count,)), dma((parts,)), dma((parts,)), dma((parts,)),
            dma((slots,)), dma((slots,)), dma((per_span,)), dma((per_span,)), dma((3,)), dma((3,)),
        ],
        compiler_params=pltpu.CompilerParams(
            collective_id=0, has_side_effects=True, vmem_limit_bytes=56 * 2**20
        ),
        cost_estimate=pl.CostEstimate(flops=6 * 10**9, bytes_accessed=5 * 10**6, transcendentals=0),
    )(
        lower_panel[0], upper_panel[0], diag_inverse[0], pivot_inverse, pattern[0], col_order,
        sep_blocks,
    )


def from_partner(value, axis, distance):
    mask = 2**distance
    pairs = [(source, source ^ mask) for source in range(lax.axis_size(axis))]
    return lax.ppermute(value, axis, pairs)


def broadcast(x, axis, root):
    mine = lax.axis_index(axis) == root
    return lax.psum(jnp.where(mine, x, jnp.zeros_like(x)), axis)


def share_rows(values, level):
    for bit in range(level + 1):
        other = from_partner(values, "layer", bit)
        values = (values.astype(jnp.float32) + other.astype(jnp.float32)).astype(jnp.bfloat16)
    return values


def shards(lower_panel, upper_panel, diag_inverse, pivot_inverse, pattern, col_order, sep_blocks):
    supernodes = diag_inverse.shape[1]
    node_width = diag_inverse.shape[2]
    local_cols = upper_panel.shape[2]
    col_index = lax.axis_index("col")
    first_col = col_index * local_cols
    nblocks = col_order.shape[0]
    solved = jnp.einsum(
        "sab,sbc->sac",
        diag_inverse[0],
        upper_panel[0].reshape(supernodes, node_width, local_cols),
        preferred_element_type=jnp.float32,
    )
    right = solved.astype(jnp.bfloat16).reshape(supernodes * node_width, local_cols)
    row_flags = jnp.repeat(pattern[0, 0], NB).astype(jnp.float32)
    all_col_flags = jnp.repeat(pattern[0, 1], NB).astype(jnp.float32)
    col_flags = lax.dynamic_slice_in_dim(all_col_flags, first_col, local_cols)
    product = jnp.dot(
        lax.all_gather(lower_panel[0], "col", axis=0, tiled=True),
        right,
        preferred_element_type=jnp.float32,
    )
    current = (-product * row_flags[:, None] * col_flags[None, :]).astype(jnp.bfloat16)
    layer_count = lax.axis_size("layer")
    layer_index = lax.axis_index("layer")
    levels = layer_count.bit_length() - 1
    positions = jnp.arange(nblocks, dtype=jnp.int32)
    total_rows = current.shape[0]
    span_rows = total_rows // layer_count
    col_blocks = (first_col + jnp.arange(local_cols, dtype=jnp.int32)) // NB
    held = current.reshape(layer_count, span_rows, local_cols)
    for level in range(levels):
        count = held.shape[0] // 2
        paired = held.reshape(count, 2, span_rows, local_cols)
        side = layer_index >> level & 1
        keep_half = lax.dynamic_index_in_dim(paired, side, 1, keepdims=False)
        send_half = lax.dynamic_index_in_dim(paired, 1 - side, 1, keepdims=False)
        partner = from_partner(send_half, "layer", level)
        total = keep_half.astype(jnp.float32) + partner.astype(jnp.float32)
        stride = 2 ** (level + 1)
        base = layer_index % stride
        span_ids = base + stride * jnp.arange(count, dtype=jnp.int32)
        global_rows = (
            span_ids[:, None] * span_rows + jnp.arange(span_rows, dtype=jnp.int32)[None, :]
        ).reshape(count * span_rows)
        separator = sep_blocks[level]
        position = jnp.sum(jnp.where(col_order == separator, positions, 0))
        owner = position * NB // local_cols
        offset = position * NB - owner * local_cols
        sep_row = separator * NB
        sep_span = sep_row // span_rows
        inner = sep_row - sep_span * span_rows
        holds = sep_span % stride == base
        local_span = jnp.where(holds, sep_span // stride, 0)
        zero = jnp.zeros((), jnp.int32)
        rows_here = lax.dynamic_slice(
            total, (local_span, inner, zero), (1, NB, local_cols)
        ).reshape(NB, local_cols)
        masked = jnp.where(holds, rows_here, jnp.zeros_like(rows_here)).astype(jnp.bfloat16)
        upper_rows = share_rows(masked, level)
        flat = total.reshape(count * span_rows, local_cols)
        local_panel = lax.dynamic_slice_in_dim(flat, offset, NB, 1).astype(jnp.bfloat16)
        local_factor = jnp.dot(
            local_panel, pivot_inverse[level], preferred_element_type=jnp.float32
        ).astype(jnp.bfloat16)
        factor = broadcast(local_factor, "col", owner)
        updated = flat - jnp.dot(factor, upper_rows, preferred_element_type=jnp.float32)
        keep = (global_rows // NB != separator)[:, None] & (col_blocks != position)[None, :]
        kept = jnp.where(keep, updated, jnp.zeros_like(updated)).astype(jnp.bfloat16)
        held = kept.reshape(count, span_rows, local_cols)
    result = held.reshape(span_rows, local_cols)
    return result


def fits(mesh, args):
    layers, columns = mesh.shape["layer"], mesh.shape["col"]
    lower_panel, upper_panel, diag_inverse = args[:3]
    rows, width = lower_panel.shape[1] // columns, lower_panel.shape[2]
    cols = upper_panel.shape[2] // columns
    return (
        layers == 4
        and columns % layers == 0
        and rows % NB == 0
        and cols % (2 * NB) == 0
        and width % (2 * NB) == 0
        and diag_inverse.shape[2] % NB == 0
    )


def solution(mesh):
    in_specs = (
        P("layer", "col", None),
        P("layer", None, "col"),
        P("layer", None, None, None),
        P(),
        P("layer", None, None),
        P(),
        P(),
    )
    out_specs = P("layer", "col")

    def run(*args):
        body = fused if fits(mesh, args) else shards
        return jax.shard_map(body, mesh=mesh, in_specs=in_specs, out_specs=out_specs, check_vma=False)(*args)

    return run
```

```python
import functools

import jax
import jax.numpy as jnp
from jax import lax
from jax.experimental import pallas as pl
from jax.experimental.pallas import tpu as pltpu
from jax.sharding import PartitionSpec as P

NB = 128
F32 = jnp.float32
BF16 = jnp.bfloat16
MESH = pl.DeviceIdType.MESH


def dot(a, b):
    return jnp.dot(a, b, preferred_element_type=F32)


def fused_kernel(
    col_count, l_ref, u_ref, d_ref, piv_ref, pat_ref, ord_ref, sep_ref, out_ref,
    lbuf, rbuf, pbuf, cin, xin, v0, vbase, vy, vr, vl, vsr, vsl, s_acc, s_own, s_core, s_tot, s_x,
    y_send, yb_send, yv_send, zr_send, zl_send, br_send, bl_send, vr_send, vl_send, l_recv, b_recv, vy_recv, vr_recv, vl_recv,
    c_send, c_recv, x_send, x_recv, s_send, s_recv,
):
    piece_rows, width = l_ref.shape
    half = piece_rows // 2
    cols = u_ref.shape[1]
    ext = rbuf.shape[1]
    nz = col_count // 2
    blocks = cols // NB
    per_half = half // NB
    few = max(piece_rows // 16, 16)
    layer = lax.axis_index("layer")
    core, xx = layer % 2, layer // 2
    ci = lax.axis_index("col")
    y, z = ci % 2, ci // 2
    core_peer = {"layer": layer + 1 - 2 * core}
    x_peer = {"layer": layer + 2 - 4 * xx}
    y_peer = {"col": ci + 1 - 2 * y}
    right, left = {"col": ci + 2}, {"col": ci - 2}
    has_right, has_left = z < nz - 1, z > 0
    first = ci * blocks

    def one_if(condition):
        return jnp.where(condition, 1.0, 0.0).astype(F32)

    def hot_row(k, block):
        return one_if(sep_ref[k] == block)

    def hot_col(k, b):
        return one_if(ord_ref[first + b] == sep_ref[k])


    def copy(src, dst, send, recv, peer):
        return pltpu.make_async_remote_copy(
            src_ref=src, dst_ref=dst, send_sem=send, recv_sem=recv, device_id=peer, device_id_type=MESH
        )

    def piece(p):
        return pl.ds(pl.multiple_of(p * piece_rows, piece_rows), piece_rows)

    def chunk(q):
        return pl.ds(pl.multiple_of(q * half, half), half)

    barrier = pltpu.get_barrier_semaphore()
    for peer in (core_peer, x_peer, y_peer):
        pl.semaphore_signal(barrier, inc=1, device_id=peer, device_id_type=MESH)

    @pl.when(has_right)
    def _():
        pl.semaphore_signal(barrier, inc=1, device_id=right, device_id_type=MESH)

    @pl.when(has_left)
    def _():
        pl.semaphore_signal(barrier, inc=1, device_id=left, device_id_type=MESH)

    for k in range(2):
        taken = u_ref[:, 0:NB].astype(F32) * hot_col(k, 0)
        for b in range(1, blocks):
            taken = taken + u_ref[:, b * NB : (b + 1) * NB].astype(F32) * hot_col(k, b)
        v0[:, k * NB : (k + 1) * NB] = taken.astype(BF16)

    pl.semaphore_wait(barrier, 3 + jnp.where(has_right, 1, 0) + jnp.where(has_left, 1, 0))

    parts = 4
    part = v0.shape[0] // parts
    y_first, z_first = (0, 1), (2, 3)

    def vpart(k):
        return pl.ds(k * part, part)

    def v_y(k):
        src = v0 if k in y_first else vbase
        return copy(src.at[vpart(k)], vy.at[vpart(k)], yv_send.at[k], vy_recv.at[k], y_peer)

    def v_right(k):
        return copy(vsr.at[vpart(k)], vr.at[vpart(k)], vr_send.at[k], vr_recv.at[k], right)

    def v_left(k):
        return copy(vsl.at[vpart(k)], vl.at[vpart(k)], vl_send.at[k], vl_recv.at[k], left)

    def add_right(k):
        rows = vpart(k)

        @pl.when(has_left)
        def _():
            v_right(k).wait_recv()
            vsr[rows, :] = vsr[rows, :] + vr[rows, :]

        @pl.when(has_right)
        def _():
            v_right(k).start()

    def add_left(k):
        rows = vpart(k)

        @pl.when(has_right)
        def _():
            v_left(k).wait_recv()
            vsl[rows, :] = vsl[rows, :] + vl[rows, :]

        @pl.when(has_left)
        def _():
            v_left(k).start()

    def near_way(k):
        pl.when(z < nz // 2)(functools.partial(add_right, k))
        pl.when(z >= nz // 2)(functools.partial(add_left, k))

    def far_way(k):
        pl.when(z < nz // 2)(functools.partial(add_left, k))
        pl.when(z >= nz // 2)(functools.partial(add_right, k))

    for k in y_first:
        v_y(k).start()
    vsr[...] = v0[...]
    vsl[...] = v0[...]

    @pl.when(z == 0)
    def _():
        for k in z_first:
            v_right(k).start()

    @pl.when(z == nz - 1)
    def _():
        for k in z_first:
            v_left(k).start()

    lbuf[piece(ci), :] = l_ref[...]

    def head(p, h):
        return pl.ds(pl.multiple_of(p * piece_rows + h * half, half), half - few * h)

    def tail(p):
        return pl.ds(pl.multiple_of(p * piece_rows + (piece_rows - few), few), few)

    def z_right(p, h):
        rows = chunk(2 * p + h)
        return copy(lbuf.at[rows], lbuf.at[rows], zr_send.at[p // 2 * 2 + h], l_recv.at[2 * p + h], right)

    def z_left(p, h):
        rows = chunk(2 * p + h)
        return copy(lbuf.at[rows], lbuf.at[rows], zl_send.at[p // 2 * 2 + h], l_recv.at[2 * p + h], left)

    def tail_right(p):
        return copy(lbuf.at[tail(p)], lbuf.at[tail(p)], br_send.at[p // 2], b_recv.at[p], right)

    def tail_left(p):
        return copy(lbuf.at[tail(p)], lbuf.at[tail(p)], bl_send.at[p // 2], b_recv.at[p], left)

    def over_y(p, h):
        rows = head(p, h)
        return copy(lbuf.at[rows], lbuf.at[rows], y_send.at[p // 2 * 2 + h], l_recv.at[2 * p + h], y_peer)

    def tail_over_y(p):
        return copy(lbuf.at[tail(p)], lbuf.at[tail(p)], yb_send.at[0], b_recv.at[p], y_peer)

    tail_over_y(ci).start()
    for h in range(2):
        over_y(ci, h).start()

    s_acc[...] = jnp.zeros_like(s_acc)

    @pl.when((z > 0) & (z < nz - 1))
    def _():
        for k in z_first:
            near_way(k)

    for k in y_first:
        rows = vpart(k)
        v_y(k).wait_recv()
        summed = v0[rows, :] + vy[rows, :]
        vbase[rows, :] = summed
        vsr[rows, :] = summed
        vsl[rows, :] = summed
        near_way(k)
    for k in z_first:
        rows = vpart(k)
        far_way(k)
        vbase[rows, :] = vsr[rows, :] + vsl[rows, :] - v0[rows, :]
        v_y(k).start()
    for k in y_first:
        far_way(k)

    for h in range(2):

        @pl.when(has_right)
        def _():
            z_right(ci, h).start()

        @pl.when(has_left)
        def _():
            z_left(ci, h).start()

    other = ci + 1 - 2 * y
    tail_over_y(other).wait_recv()

    @pl.when(has_right)
    def _():
        tail_right(other).start()

    @pl.when(has_left)
    def _():
        tail_left(other).start()

    supers, node = d_ref.shape[0], d_ref.shape[1]
    for s in range(supers):
        solved = dot(d_ref[s], u_ref[s * node : (s + 1) * node, :])
        rounded = solved.astype(BF16).astype(F32)
        for b in range(blocks):
            flag = -pat_ref[1, first + b].astype(F32)
            rbuf[s * node : (s + 1) * node, b * NB : (b + 1) * NB] = (
                rounded[:, b * NB : (b + 1) * NB] * flag
            ).astype(BF16)

    for k in z_first:
        rows = vpart(k)
        v_y(k).wait_recv()
        v0[rows, :] = vbase[rows, :] + vy[rows, :]
    for k in y_first:
        rows = vpart(k)
        v_y(k).wait_send()
        v0[rows, :] = vsr[rows, :] + vsl[rows, :] - vbase[rows, :]
    for s in range(supers):
        solved = dot(d_ref[s], v0[s * node : (s + 1) * node, :])
        rounded = solved.astype(BF16).astype(F32)
        for k in range(2):
            held = jnp.int32(0)
            for p in range(ord_ref.shape[0]):
                held = held + jnp.where(ord_ref[p] == sep_ref[k], pat_ref[1, p], 0)
            rbuf[s * node : (s + 1) * node, cols + k * NB : cols + (k + 1) * NB] = (
                rounded[:, k * NB : (k + 1) * NB] * -held.astype(F32)
            ).astype(BF16)

    per_span = col_count // 4

    span_halves = 2 * per_span

    def slot_of(q):
        return q // span_halves // 2 * span_halves + q % span_halves

    def to_core(q):
        slot = slot_of(q)
        return copy(pbuf.at[chunk(q)], cin.at[slot], c_send.at[slot], c_recv.at[slot], core_peer)

    def to_x(q):
        slot = q % span_halves
        return copy(pbuf.at[chunk(q)], xin.at[slot], x_send.at[slot], x_recv.at[slot], x_peer)

    def process(q):
        rows = lbuf[chunk(q), :]
        for n in range(0, ext, 2 * NB):
            acc = dot(rows, rbuf[:, n : n + 2 * NB])
            found = [None, None]
            for j in range(per_half):
                block = q * per_half + j
                flagged = acc[j * NB : (j + 1) * NB] * pat_ref[0, block].astype(F32)
                pbuf[pl.ds(pl.multiple_of(block * NB, NB), NB), n : n + 2 * NB] = flagged.astype(BF16)
                for k in range(2):
                    term = flagged * hot_row(k, block)
                    found[k] = term if j == 0 else found[k] + term
            for k in range(2):
                s_acc[k * NB : (k + 1) * NB, n : n + 2 * NB] += found[k]
        span = q // span_halves

        @pl.when(span % 2 != core)
        def _():
            to_core(q).start()

    def finish(q):
        span = q // span_halves

        @pl.when(span % 2 == core)
        def _():
            to_core(q).wait_recv()
            slot = slot_of(q)

            @pl.loop(0, per_half)
            def _(j):
                at = pl.ds(pl.multiple_of(q * half + j * NB, NB), NB)
                here = pl.ds(pl.multiple_of(j * NB, NB), NB)
                pbuf[at, :] = (pbuf[at, :].astype(F32) + cin[slot, here, :].astype(F32)).astype(BF16)

            @pl.when(span // 2 != xx)
            def _():
                to_x(q).start()

    @pl.loop(0, nz)
    def _(step):
        for h in range(2):
            for way in (1, -1):
                zc = z + way * (step + 1)

                @pl.when((zc >= 0) & (zc < nz))
                def _(zc=zc, way=way, h=h):
                    p, o = zc * 2 + y, zc * 2 + 1 - y
                    z_right(p, h).wait_recv()
                    on = has_left if way > 0 else has_right

                    @pl.when(on)
                    def _():
                        (z_left if way > 0 else z_right)(p, h).start()

                    over_y(p, h).start()
                    if h == 1:
                        tail_right(o).wait_recv()

                        @pl.when(on)
                        def _():
                            (tail_left if way > 0 else tail_right)(o).start()

        def candidate(t):
            zc = z + step * (1 - 2 * (t % 2))
            line = jnp.where(t < 4, y, 1 - y)
            valid = (zc >= 0) & (zc < nz) & ((step > 0) | (t % 2 == 0))
            return zc * 2 + line, (t // 2) % 2, valid

        @pl.loop(0, 9)
        def _(t):
            p, h, valid = candidate(t)

            @pl.when((t < 8) & valid)
            def _():
                @pl.when((t >= 4) & (h == 0))
                def _():
                    over_y(p, 0).wait_recv()

                @pl.when((t >= 4) & (h == 1))
                def _():
                    over_y(p, 1).wait_recv()

                process(2 * p + h)

            p_before, h_before, valid_before = candidate(jnp.maximum(t - 1, 0))

            @pl.when((t > 0) & valid_before)
            def _():
                finish(2 * p_before + h_before)

    def s_copy(src, dst, k, peer):
        return copy(src, dst, s_send.at[k], s_recv.at[k], peer)

    s_own[...] = s_acc[...].astype(BF16)
    swap = s_copy(s_own, s_core, 0, core_peer)
    swap.start()
    swap.wait()
    s_tot[...] = (s_own[...].astype(F32) + s_core[...].astype(F32)).astype(BF16)
    mine = pl.ds(pl.multiple_of(core * NB, NB), NB)
    over_x = s_copy(s_tot.at[mine], s_x.at[mine], 1, x_peer)
    over_x.start()
    over_x.wait_recv()
    share = s_copy(s_x.at[mine], s_x.at[mine], 2, core_peer)
    share.start()
    share.wait_recv()

    pos_col = [cols, cols + NB]
    upper = jnp.concatenate([s_tot[0:NB, 0:cols], s_x[0:NB, 0:cols]], axis=0)
    upper_p = jnp.concatenate([s_tot[0:NB, pos_col[1] : ext], s_x[0:NB, pos_col[1] : ext]], axis=0)
    keep_c = [
        jnp.concatenate([jnp.full((1, NB), 1.0, F32) * (1.0 - hot_col(k, b)) for b in range(blocks)], axis=1)
        for k in range(2)
    ]

    def factors(a, b):
        return jnp.concatenate([dot(a, piv_ref[0]).astype(BF16), dot(b, piv_ref[0]).astype(BF16)], axis=1)

    fs = factors(s_tot[NB : 2 * NB, cols : cols + NB], s_x[NB : 2 * NB, cols : cols + NB])
    last = s_tot[NB : 2 * NB, 0:cols].astype(F32) + s_x[NB : 2 * NB, 0:cols].astype(F32)
    upper2 = ((last - dot(fs, upper)) * keep_c[0]).astype(BF16)

    for slot in range(span_halves):
        q = layer * span_halves + slot

        to_x(q).wait_recv()
        at = chunk(q)
        f0 = factors(pbuf[at, cols : cols + NB], xin[slot, :, cols : cols + NB])

        def keep_rows(value, k):
            kept = [
                value[j * NB : (j + 1) * NB] * (1.0 - hot_row(k, q * per_half + j)) for j in range(per_half)
            ]
            return jnp.concatenate(kept, axis=0)

        panel = pbuf[at, pos_col[1] : ext].astype(F32) + xin[slot, :, pos_col[1] : ext].astype(F32)
        panel = keep_rows(panel - dot(f0, upper_p), 0).astype(BF16)
        f2 = dot(panel, piv_ref[1]).astype(BF16)
        total = pbuf[at, 0:cols].astype(F32) + xin[slot, :, 0:cols].astype(F32)
        total = keep_rows(total - dot(f0, upper), 0) * keep_c[0]
        final = keep_rows(total - dot(f2, upper2), 1) * keep_c[1]
        out_ref[slot * half : (slot + 1) * half, :] = final.astype(BF16)

    over_x.wait_send()
    share.wait_send()
    for k in range(parts):
        if k in z_first:
            v_y(k).wait_send()

        @pl.when(has_right)
        def _():
            v_right(k).wait_send()

        @pl.when(has_left)
        def _():
            v_left(k).wait_send()

    tail_over_y(ci).wait_send()

    @pl.loop(0, nz)
    def _(zc):
        p, o = zc * 2 + y, zc * 2 + 1 - y
        for h in range(2):
            over_y(p, h).wait_send()

            @pl.when(has_right & (zc <= z))
            def _():
                z_right(p, h).wait_send()

            @pl.when(has_left & (zc >= z))
            def _():
                z_left(p, h).wait_send()

        @pl.when(has_right & (zc <= z))
        def _():
            tail_right(o).wait_send()

        @pl.when(has_left & (zc >= z))
        def _():
            tail_left(o).wait_send()

    @pl.loop(0, 2 * col_count)
    def _(q):
        span = q // span_halves

        @pl.when(span % 2 != core)
        def _():
            to_core(q).wait_send()

        @pl.when((span % 2 == core) & (span // 2 != xx))
        def _():
            to_x(q).wait_send()


def fused(lower_panel, upper_panel, diag_inverse, pivot_inverse, pattern, col_order, sep_blocks):
    col_count = lax.axis_size("col")
    piece_rows, width = lower_panel.shape[1:]
    cols = upper_panel.shape[2]
    ext = cols + 2 * NB
    nz, slots, half = col_count // 2, col_count, piece_rows // 2
    total_rows = piece_rows * col_count
    per_span = col_count // 4
    parts = 4
    vmem = pl.BlockSpec(memory_space=pltpu.VMEM)
    smem = pl.BlockSpec(memory_space=pltpu.SMEM)
    dma = pltpu.SemaphoreType.DMA
    v_shape = pltpu.VMEM((width, 2 * NB), BF16)
    s_shape = pltpu.VMEM((2 * NB, ext), BF16)
    return pl.pallas_call(
        functools.partial(fused_kernel, col_count),
        out_shape=jax.ShapeDtypeStruct((per_span * piece_rows, cols), BF16),
        in_specs=[vmem] * 4 + [smem] * 3,
        out_specs=vmem,
        scratch_shapes=[
            pltpu.VMEM((total_rows, width), BF16),
            pltpu.VMEM((width, ext), BF16),
            pltpu.VMEM((total_rows, ext), BF16),
            pltpu.VMEM((slots, half, ext), BF16),
            pltpu.VMEM((2 * per_span, half, ext), BF16),
            v_shape, v_shape, v_shape, v_shape, v_shape, v_shape, v_shape,
            pltpu.VMEM((2 * NB, ext), F32), s_shape, s_shape, s_shape, s_shape,
            dma((2 * nz,)), dma((1,)), dma((parts,)), dma((2 * nz,)), dma((2 * nz,)), dma((nz,)), dma((nz,)), dma((parts,)), dma((parts,)),
            dma((2 * col_count,)), dma((col_count,)), dma((parts,)), dma((parts,)), dma((parts,)),
            dma((slots,)), dma((slots,)), dma((2 * per_span,)), dma((2 * per_span,)), dma((3,)), dma((3,)),
        ],
        compiler_params=pltpu.CompilerParams(
            collective_id=0, has_side_effects=True, vmem_limit_bytes=56 * 2**20
        ),
        cost_estimate=pl.CostEstimate(flops=6 * 10**9, bytes_accessed=5 * 10**6, transcendentals=0),
    )(
        lower_panel[0], upper_panel[0], diag_inverse[0], pivot_inverse, pattern[0], col_order,
        sep_blocks,
    )


def from_partner(value, axis, distance):
    mask = 2**distance
    pairs = [(source, source ^ mask) for source in range(lax.axis_size(axis))]
    return lax.ppermute(value, axis, pairs)


def broadcast(x, axis, root):
    mine = lax.axis_index(axis) == root
    return lax.psum(jnp.where(mine, x, jnp.zeros_like(x)), axis)


def share_rows(values, level):
    for bit in range(level + 1):
        other = from_partner(values, "layer", bit)
        values = (values.astype(jnp.float32) + other.astype(jnp.float32)).astype(jnp.bfloat16)
    return values


def shards(lower_panel, upper_panel, diag_inverse, pivot_inverse, pattern, col_order, sep_blocks):
    supernodes = diag_inverse.shape[1]
    node_width = diag_inverse.shape[2]
    local_cols = upper_panel.shape[2]
    col_index = lax.axis_index("col")
    first_col = col_index * local_cols
    nblocks = col_order.shape[0]
    solved = jnp.einsum(
        "sab,sbc->sac",
        diag_inverse[0],
        upper_panel[0].reshape(supernodes, node_width, local_cols),
        preferred_element_type=jnp.float32,
    )
    right = solved.astype(jnp.bfloat16).reshape(supernodes * node_width, local_cols)
    row_flags = jnp.repeat(pattern[0, 0], NB).astype(jnp.float32)
    all_col_flags = jnp.repeat(pattern[0, 1], NB).astype(jnp.float32)
    col_flags = lax.dynamic_slice_in_dim(all_col_flags, first_col, local_cols)
    product = jnp.dot(
        lax.all_gather(lower_panel[0], "col", axis=0, tiled=True),
        right,
        preferred_element_type=jnp.float32,
    )
    current = (-product * row_flags[:, None] * col_flags[None, :]).astype(jnp.bfloat16)
    layer_count = lax.axis_size("layer")
    layer_index = lax.axis_index("layer")
    levels = layer_count.bit_length() - 1
    positions = jnp.arange(nblocks, dtype=jnp.int32)
    total_rows = current.shape[0]
    span_rows = total_rows // layer_count
    col_blocks = (first_col + jnp.arange(local_cols, dtype=jnp.int32)) // NB
    held = current.reshape(layer_count, span_rows, local_cols)
    for level in range(levels):
        count = held.shape[0] // 2
        paired = held.reshape(count, 2, span_rows, local_cols)
        side = layer_index >> level & 1
        keep_half = lax.dynamic_index_in_dim(paired, side, 1, keepdims=False)
        send_half = lax.dynamic_index_in_dim(paired, 1 - side, 1, keepdims=False)
        partner = from_partner(send_half, "layer", level)
        total = keep_half.astype(jnp.float32) + partner.astype(jnp.float32)
        stride = 2 ** (level + 1)
        base = layer_index % stride
        span_ids = base + stride * jnp.arange(count, dtype=jnp.int32)
        global_rows = (
            span_ids[:, None] * span_rows + jnp.arange(span_rows, dtype=jnp.int32)[None, :]
        ).reshape(count * span_rows)
        separator = sep_blocks[level]
        position = jnp.sum(jnp.where(col_order == separator, positions, 0))
        owner = position * NB // local_cols
        offset = position * NB - owner * local_cols
        sep_row = separator * NB
        sep_span = sep_row // span_rows
        inner = sep_row - sep_span * span_rows
        holds = sep_span % stride == base
        local_span = jnp.where(holds, sep_span // stride, 0)
        zero = jnp.zeros((), jnp.int32)
        rows_here = lax.dynamic_slice(
            total, (local_span, inner, zero), (1, NB, local_cols)
        ).reshape(NB, local_cols)
        masked = jnp.where(holds, rows_here, jnp.zeros_like(rows_here)).astype(jnp.bfloat16)
        upper_rows = share_rows(masked, level)
        flat = total.reshape(count * span_rows, local_cols)
        local_panel = lax.dynamic_slice_in_dim(flat, offset, NB, 1).astype(jnp.bfloat16)
        local_factor = jnp.dot(
            local_panel, pivot_inverse[level], preferred_element_type=jnp.float32
        ).astype(jnp.bfloat16)
        factor = broadcast(local_factor, "col", owner)
        updated = flat - jnp.dot(factor, upper_rows, preferred_element_type=jnp.float32)
        keep = (global_rows // NB != separator)[:, None] & (col_blocks != position)[None, :]
        kept = jnp.where(keep, updated, jnp.zeros_like(updated)).astype(jnp.bfloat16)
        held = kept.reshape(count, span_rows, local_cols)
    result = held.reshape(span_rows, local_cols)
    return result


def fits(mesh, args):
    layers, columns = mesh.shape["layer"], mesh.shape["col"]
    lower_panel, upper_panel, diag_inverse = args[:3]
    rows, width = lower_panel.shape[1] // columns, lower_panel.shape[2]
    cols = upper_panel.shape[2] // columns
    return (
        layers == 4
        and columns % layers == 0
        and rows % (2 * NB) == 0
        and cols % (2 * NB) == 0
        and width % (2 * NB) == 0
        and diag_inverse.shape[2] % NB == 0
    )


def solution(mesh):
    in_specs = (
        P("layer", "col", None),
        P("layer", None, "col"),
        P("layer", None, None, None),
        P(),
        P("layer", None, None),
        P(),
        P(),
    )
    out_specs = P("layer", "col")

    def run(*args):
        body = fused if fits(mesh, args) else shards
        return jax.shard_map(body, mesh=mesh, in_specs=in_specs, out_specs=out_specs, check_vma=False)(*args)

    return run
```

```python
import functools

import jax
import jax.numpy as jnp
from jax import lax
from jax.experimental import pallas as pl
from jax.experimental.pallas import tpu as pltpu
from jax.sharding import PartitionSpec as P

NB = 128
F32 = jnp.float32
BF16 = jnp.bfloat16
MESH = pl.DeviceIdType.MESH


def dot(a, b):
    return jnp.dot(a, b, preferred_element_type=F32)


def fused_kernel(
    col_count, l_ref, u_ref, d_ref, piv_ref, pat_ref, ord_ref, sep_ref, out_ref,
    lbuf, rbuf, pbuf, cin, xin, v0, vbase, vy, vr, vl, vsr, vsl, s_acc, s_own, s_core, s_tot, s_x,
    y_send, yb_send, yv_send, zr_send, zl_send, br_send, bl_send, vr_send, vl_send, l_recv, b_recv, vy_recv, vr_recv, vl_recv,
    c_send, c_recv, x_send, x_recv, s_send, s_recv,
):
    piece_rows, width = l_ref.shape
    half = piece_rows // 2
    cols = u_ref.shape[1]
    ext = rbuf.shape[1]
    nz = col_count // 2
    blocks = cols // NB
    per_half = half // NB
    few = max(piece_rows // 16, 16)
    layer = lax.axis_index("layer")
    core, xx = layer % 2, layer // 2
    ci = lax.axis_index("col")
    y, z = ci % 2, ci // 2
    core_peer = {"layer": layer + 1 - 2 * core}
    x_peer = {"layer": layer + 2 - 4 * xx}
    y_peer = {"col": ci + 1 - 2 * y}
    right, left = {"col": ci + 2}, {"col": ci - 2}
    has_right, has_left = z < nz - 1, z > 0
    first = ci * blocks

    def one_if(condition):
        return jnp.where(condition, 1.0, 0.0).astype(F32)

    def hot_row(k, block):
        return one_if(sep_ref[k] == block)

    def hot_col(k, b):
        return one_if(ord_ref[first + b] == sep_ref[k])


    def copy(src, dst, send, recv, peer):
        return pltpu.make_async_remote_copy(
            src_ref=src, dst_ref=dst, send_sem=send, recv_sem=recv, device_id=peer, device_id_type=MESH
        )

    def piece(p):
        return pl.ds(pl.multiple_of(p * piece_rows, piece_rows), piece_rows)

    def chunk(q):
        return pl.ds(pl.multiple_of(q * half, half), half)

    barrier = pltpu.get_barrier_semaphore()
    for peer in (core_peer, x_peer, y_peer):
        pl.semaphore_signal(barrier, inc=1, device_id=peer, device_id_type=MESH)

    @pl.when(has_right)
    def _():
        pl.semaphore_signal(barrier, inc=1, device_id=right, device_id_type=MESH)

    @pl.when(has_left)
    def _():
        pl.semaphore_signal(barrier, inc=1, device_id=left, device_id_type=MESH)

    for k in range(2):
        taken = u_ref[:, 0:NB].astype(F32) * hot_col(k, 0)
        for b in range(1, blocks):
            taken = taken + u_ref[:, b * NB : (b + 1) * NB].astype(F32) * hot_col(k, b)
        v0[:, k * NB : (k + 1) * NB] = taken.astype(BF16)

    pl.semaphore_wait(barrier, 3 + jnp.where(has_right, 1, 0) + jnp.where(has_left, 1, 0))

    parts = 4
    part = v0.shape[0] // parts
    y_first, z_first = (0, 1), (2, 3)

    def vpart(k):
        return pl.ds(k * part, part)

    def v_y(k):
        src = v0 if k in y_first else vbase
        return copy(src.at[vpart(k)], vy.at[vpart(k)], yv_send.at[k], vy_recv.at[k], y_peer)

    def v_right(k):
        return copy(vsr.at[vpart(k)], vr.at[vpart(k)], vr_send.at[k], vr_recv.at[k], right)

    def v_left(k):
        return copy(vsl.at[vpart(k)], vl.at[vpart(k)], vl_send.at[k], vl_recv.at[k], left)

    def add_right(k):
        rows = vpart(k)

        @pl.when(has_left)
        def _():
            v_right(k).wait_recv()
            vsr[rows, :] = vsr[rows, :] + vr[rows, :]

        @pl.when(has_right)
        def _():
            v_right(k).start()

    def add_left(k):
        rows = vpart(k)

        @pl.when(has_right)
        def _():
            v_left(k).wait_recv()
            vsl[rows, :] = vsl[rows, :] + vl[rows, :]

        @pl.when(has_left)
        def _():
            v_left(k).start()

    def near_way(k):
        pl.when(z < nz // 2)(functools.partial(add_right, k))
        pl.when(z >= nz // 2)(functools.partial(add_left, k))

    def far_way(k):
        pl.when(z < nz // 2)(functools.partial(add_left, k))
        pl.when(z >= nz // 2)(functools.partial(add_right, k))

    for k in y_first:
        v_y(k).start()
    vsr[...] = v0[...]
    vsl[...] = v0[...]

    @pl.when(z == 0)
    def _():
        for k in z_first:
            v_right(k).start()

    @pl.when(z == nz - 1)
    def _():
        for k in z_first:
            v_left(k).start()

    lbuf[piece(ci), :] = l_ref[...]

    def head(p, h):
        return pl.ds(pl.multiple_of(p * piece_rows + h * half, half), half - few * h)

    def tail(p):
        return pl.ds(pl.multiple_of(p * piece_rows + (piece_rows - few), few), few)

    def z_right(p, h):
        rows = chunk(2 * p + h)
        return copy(lbuf.at[rows], lbuf.at[rows], zr_send.at[p // 2 * 2 + h], l_recv.at[2 * p + h], right)

    def z_left(p, h):
        rows = chunk(2 * p + h)
        return copy(lbuf.at[rows], lbuf.at[rows], zl_send.at[p // 2 * 2 + h], l_recv.at[2 * p + h], left)

    def tail_right(p):
        return copy(lbuf.at[tail(p)], lbuf.at[tail(p)], br_send.at[p // 2], b_recv.at[p], right)

    def tail_left(p):
        return copy(lbuf.at[tail(p)], lbuf.at[tail(p)], bl_send.at[p // 2], b_recv.at[p], left)

    def over_y(p, h):
        rows = head(p, h)
        return copy(lbuf.at[rows], lbuf.at[rows], y_send.at[p // 2 * 2 + h], l_recv.at[2 * p + h], y_peer)

    def tail_over_y(p):
        return copy(lbuf.at[tail(p)], lbuf.at[tail(p)], yb_send.at[0], b_recv.at[p], y_peer)

    tail_over_y(ci).start()
    for h in range(2):
        over_y(ci, h).start()

    s_acc[...] = jnp.zeros_like(s_acc)

    @pl.when((z > 0) & (z < nz - 1))
    def _():
        for k in z_first:
            near_way(k)

    for k in y_first:
        rows = vpart(k)
        v_y(k).wait_recv()
        summed = v0[rows, :] + vy[rows, :]
        vbase[rows, :] = summed
        vsr[rows, :] = summed
        vsl[rows, :] = summed
        near_way(k)
    for k in z_first:
        rows = vpart(k)
        far_way(k)
        vbase[rows, :] = vsr[rows, :] + vsl[rows, :] - v0[rows, :]
        v_y(k).start()
    for k in y_first:
        far_way(k)

    for h in range(2):

        @pl.when(has_right)
        def _():
            z_right(ci, h).start()

        @pl.when(has_left)
        def _():
            z_left(ci, h).start()

    other = ci + 1 - 2 * y
    tail_over_y(other).wait_recv()

    @pl.when(has_right)
    def _():
        tail_right(other).start()

    @pl.when(has_left)
    def _():
        tail_left(other).start()

    supers, node = d_ref.shape[0], d_ref.shape[1]
    for s in range(supers):
        solved = dot(d_ref[s], u_ref[s * node : (s + 1) * node, :])
        rounded = solved.astype(BF16).astype(F32)
        for b in range(blocks):
            flag = -pat_ref[1, first + b].astype(F32)
            rbuf[s * node : (s + 1) * node, b * NB : (b + 1) * NB] = (
                rounded[:, b * NB : (b + 1) * NB] * flag
            ).astype(BF16)

    for k in z_first:
        rows = vpart(k)
        v_y(k).wait_recv()
        v0[rows, :] = vbase[rows, :] + vy[rows, :]
    for k in y_first:
        rows = vpart(k)
        v_y(k).wait_send()
        v0[rows, :] = vsr[rows, :] + vsl[rows, :] - vbase[rows, :]
    for s in range(supers):
        solved = dot(d_ref[s], v0[s * node : (s + 1) * node, :])
        rounded = solved.astype(BF16).astype(F32)
        for k in range(2):
            held = jnp.int32(0)
            for p in range(ord_ref.shape[0]):
                held = held + jnp.where(ord_ref[p] == sep_ref[k], pat_ref[1, p], 0)
            rbuf[s * node : (s + 1) * node, cols + k * NB : cols + (k + 1) * NB] = (
                rounded[:, k * NB : (k + 1) * NB] * -held.astype(F32)
            ).astype(BF16)

    per_span = col_count // 4

    span_halves = 2 * per_span

    def slot_of(q):
        return q // span_halves // 2 * span_halves + q % span_halves

    def to_core(q):
        slot = slot_of(q)
        return copy(pbuf.at[chunk(q)], cin.at[slot], c_send.at[slot], c_recv.at[slot], core_peer)

    def to_x(q):
        slot = q % span_halves
        return copy(pbuf.at[chunk(q)], xin.at[slot], x_send.at[slot], x_recv.at[slot], x_peer)

    def process(q):
        rows = lbuf[chunk(q), :]
        for n in range(0, ext, 2 * NB):
            acc = dot(rows, rbuf[:, n : n + 2 * NB])
            found = [None, None]
            for j in range(per_half):
                block = q * per_half + j
                flagged = acc[j * NB : (j + 1) * NB] * pat_ref[0, block].astype(F32)
                pbuf[pl.ds(pl.multiple_of(block * NB, NB), NB), n : n + 2 * NB] = flagged.astype(BF16)
                for k in range(2):
                    term = flagged * hot_row(k, block)
                    found[k] = term if j == 0 else found[k] + term
            for k in range(2):
                s_acc[k * NB : (k + 1) * NB, n : n + 2 * NB] += found[k]
        span = q // span_halves

        @pl.when(span % 2 != core)
        def _():
            to_core(q).start()

    def finish(q):
        span = q // span_halves

        @pl.when(span % 2 == core)
        def _():
            to_core(q).wait_recv()
            slot = slot_of(q)

            @pl.loop(0, per_half)
            def _(j):
                at = pl.ds(pl.multiple_of(q * half + j * NB, NB), NB)
                here = pl.ds(pl.multiple_of(j * NB, NB), NB)
                pbuf[at, :] = (pbuf[at, :].astype(F32) + cin[slot, here, :].astype(F32)).astype(BF16)

            @pl.when(span // 2 != xx)
            def _():
                to_x(q).start()

    def handle(step, line, arriving):
        def candidate(t):
            zc = z + step * (1 - 2 * (t % 2))
            valid = (zc >= 0) & (zc < nz) & ((step > 0) | (t % 2 == 0))
            return zc * 2 + line, t // 2, valid

        @pl.loop(0, 6)
        def _(t):
            p, h, valid = candidate(t)

            @pl.when((t < 4) & valid)
            def _():
                if arriving:

                    @pl.when(h == 0)
                    def _():
                        over_y(p, 0).wait_recv()

                    @pl.when(h == 1)
                    def _():
                        over_y(p, 1).wait_recv()

                process(2 * p + h)

            p_before, h_before, valid_before = candidate(jnp.maximum(t - 2, 0))

            @pl.when((t >= 2) & valid_before)
            def _():
                finish(2 * p_before + h_before)

    @pl.loop(0, nz)
    def _(step):
        handle(step, y, False)

        for h in range(2):
            for way in (1, -1):
                zc = z + way * (step + 1)

                @pl.when((zc >= 0) & (zc < nz))
                def _(zc=zc, way=way, h=h):
                    p, o = zc * 2 + y, zc * 2 + 1 - y
                    z_right(p, h).wait_recv()
                    on = has_left if way > 0 else has_right

                    @pl.when(on)
                    def _():
                        (z_left if way > 0 else z_right)(p, h).start()

                    over_y(p, h).start()
                    if h == 1:
                        tail_right(o).wait_recv()

                        @pl.when(on)
                        def _():
                            (tail_left if way > 0 else tail_right)(o).start()

        handle(step, 1 - y, True)

    def s_copy(src, dst, k, peer):
        return copy(src, dst, s_send.at[k], s_recv.at[k], peer)

    s_own[...] = s_acc[...].astype(BF16)
    swap = s_copy(s_own, s_core, 0, core_peer)
    swap.start()
    swap.wait()
    s_tot[...] = (s_own[...].astype(F32) + s_core[...].astype(F32)).astype(BF16)
    mine = pl.ds(pl.multiple_of(core * NB, NB), NB)
    over_x = s_copy(s_tot.at[mine], s_x.at[mine], 1, x_peer)
    over_x.start()
    over_x.wait_recv()
    share = s_copy(s_x.at[mine], s_x.at[mine], 2, core_peer)
    share.start()
    share.wait_recv()

    pos_col = [cols, cols + NB]
    upper = jnp.concatenate([s_tot[0:NB, 0:cols], s_x[0:NB, 0:cols]], axis=0)
    upper_p = jnp.concatenate([s_tot[0:NB, pos_col[1] : ext], s_x[0:NB, pos_col[1] : ext]], axis=0)
    keep_c = [
        jnp.concatenate([jnp.full((1, NB), 1.0, F32) * (1.0 - hot_col(k, b)) for b in range(blocks)], axis=1)
        for k in range(2)
    ]

    def factors(a, b):
        return jnp.concatenate([dot(a, piv_ref[0]).astype(BF16), dot(b, piv_ref[0]).astype(BF16)], axis=1)

    fs = factors(s_tot[NB : 2 * NB, cols : cols + NB], s_x[NB : 2 * NB, cols : cols + NB])
    last = s_tot[NB : 2 * NB, 0:cols].astype(F32) + s_x[NB : 2 * NB, 0:cols].astype(F32)
    upper2 = ((last - dot(fs, upper)) * keep_c[0]).astype(BF16)

    for slot in range(span_halves):
        q = layer * span_halves + slot

        to_x(q).wait_recv()
        at = chunk(q)
        f0 = factors(pbuf[at, cols : cols + NB], xin[slot, :, cols : cols + NB])

        def keep_rows(value, k):
            kept = [
                value[j * NB : (j + 1) * NB] * (1.0 - hot_row(k, q * per_half + j)) for j in range(per_half)
            ]
            return jnp.concatenate(kept, axis=0)

        panel = pbuf[at, pos_col[1] : ext].astype(F32) + xin[slot, :, pos_col[1] : ext].astype(F32)
        panel = keep_rows(panel - dot(f0, upper_p), 0).astype(BF16)
        f2 = dot(panel, piv_ref[1]).astype(BF16)
        total = pbuf[at, 0:cols].astype(F32) + xin[slot, :, 0:cols].astype(F32)
        total = keep_rows(total - dot(f0, upper), 0) * keep_c[0]
        final = keep_rows(total - dot(f2, upper2), 1) * keep_c[1]
        out_ref[slot * half : (slot + 1) * half, :] = final.astype(BF16)

    over_x.wait_send()
    share.wait_send()
    for k in range(parts):
        if k in z_first:
            v_y(k).wait_send()

        @pl.when(has_right)
        def _():
            v_right(k).wait_send()

        @pl.when(has_left)
        def _():
            v_left(k).wait_send()

    tail_over_y(ci).wait_send()

    @pl.loop(0, nz)
    def _(zc):
        p, o = zc * 2 + y, zc * 2 + 1 - y
        for h in range(2):
            over_y(p, h).wait_send()

            @pl.when(has_right & (zc <= z))
            def _():
                z_right(p, h).wait_send()

            @pl.when(has_left & (zc >= z))
            def _():
                z_left(p, h).wait_send()

        @pl.when(has_right & (zc <= z))
        def _():
            tail_right(o).wait_send()

        @pl.when(has_left & (zc >= z))
        def _():
            tail_left(o).wait_send()

    @pl.loop(0, 2 * col_count)
    def _(q):
        span = q // span_halves

        @pl.when(span % 2 != core)
        def _():
            to_core(q).wait_send()

        @pl.when((span % 2 == core) & (span // 2 != xx))
        def _():
            to_x(q).wait_send()


def fused(lower_panel, upper_panel, diag_inverse, pivot_inverse, pattern, col_order, sep_blocks):
    col_count = lax.axis_size("col")
    piece_rows, width = lower_panel.shape[1:]
    cols = upper_panel.shape[2]
    ext = cols + 2 * NB
    nz, slots, half = col_count // 2, col_count, piece_rows // 2
    total_rows = piece_rows * col_count
    per_span = col_count // 4
    parts = 4
    vmem = pl.BlockSpec(memory_space=pltpu.VMEM)
    smem = pl.BlockSpec(memory_space=pltpu.SMEM)
    dma = pltpu.SemaphoreType.DMA
    v_shape = pltpu.VMEM((width, 2 * NB), BF16)
    s_shape = pltpu.VMEM((2 * NB, ext), BF16)
    return pl.pallas_call(
        functools.partial(fused_kernel, col_count),
        out_shape=jax.ShapeDtypeStruct((per_span * piece_rows, cols), BF16),
        in_specs=[vmem] * 4 + [smem] * 3,
        out_specs=vmem,
        scratch_shapes=[
            pltpu.VMEM((total_rows, width), BF16),
            pltpu.VMEM((width, ext), BF16),
            pltpu.VMEM((total_rows, ext), BF16),
            pltpu.VMEM((slots, half, ext), BF16),
            pltpu.VMEM((2 * per_span, half, ext), BF16),
            v_shape, v_shape, v_shape, v_shape, v_shape, v_shape, v_shape,
            pltpu.VMEM((2 * NB, ext), F32), s_shape, s_shape, s_shape, s_shape,
            dma((2 * nz,)), dma((1,)), dma((parts,)), dma((2 * nz,)), dma((2 * nz,)), dma((nz,)), dma((nz,)), dma((parts,)), dma((parts,)),
            dma((2 * col_count,)), dma((col_count,)), dma((parts,)), dma((parts,)), dma((parts,)),
            dma((slots,)), dma((slots,)), dma((2 * per_span,)), dma((2 * per_span,)), dma((3,)), dma((3,)),
        ],
        compiler_params=pltpu.CompilerParams(
            collective_id=0, has_side_effects=True, vmem_limit_bytes=56 * 2**20
        ),
        cost_estimate=pl.CostEstimate(flops=6 * 10**9, bytes_accessed=5 * 10**6, transcendentals=0),
    )(
        lower_panel[0], upper_panel[0], diag_inverse[0], pivot_inverse, pattern[0], col_order,
        sep_blocks,
    )


def from_partner(value, axis, distance):
    mask = 2**distance
    pairs = [(source, source ^ mask) for source in range(lax.axis_size(axis))]
    return lax.ppermute(value, axis, pairs)


def broadcast(x, axis, root):
    mine = lax.axis_index(axis) == root
    return lax.psum(jnp.where(mine, x, jnp.zeros_like(x)), axis)


def share_rows(values, level):
    for bit in range(level + 1):
        other = from_partner(values, "layer", bit)
        values = (values.astype(jnp.float32) + other.astype(jnp.float32)).astype(jnp.bfloat16)
    return values


def shards(lower_panel, upper_panel, diag_inverse, pivot_inverse, pattern, col_order, sep_blocks):
    supernodes = diag_inverse.shape[1]
    node_width = diag_inverse.shape[2]
    local_cols = upper_panel.shape[2]
    col_index = lax.axis_index("col")
    first_col = col_index * local_cols
    nblocks = col_order.shape[0]
    solved = jnp.einsum(
        "sab,sbc->sac",
        diag_inverse[0],
        upper_panel[0].reshape(supernodes, node_width, local_cols),
        preferred_element_type=jnp.float32,
    )
    right = solved.astype(jnp.bfloat16).reshape(supernodes * node_width, local_cols)
    row_flags = jnp.repeat(pattern[0, 0], NB).astype(jnp.float32)
    all_col_flags = jnp.repeat(pattern[0, 1], NB).astype(jnp.float32)
    col_flags = lax.dynamic_slice_in_dim(all_col_flags, first_col, local_cols)
    product = jnp.dot(
        lax.all_gather(lower_panel[0], "col", axis=0, tiled=True),
        right,
        preferred_element_type=jnp.float32,
    )
    current = (-product * row_flags[:, None] * col_flags[None, :]).astype(jnp.bfloat16)
    layer_count = lax.axis_size("layer")
    layer_index = lax.axis_index("layer")
    levels = layer_count.bit_length() - 1
    positions = jnp.arange(nblocks, dtype=jnp.int32)
    total_rows = current.shape[0]
    span_rows = total_rows // layer_count
    col_blocks = (first_col + jnp.arange(local_cols, dtype=jnp.int32)) // NB
    held = current.reshape(layer_count, span_rows, local_cols)
    for level in range(levels):
        count = held.shape[0] // 2
        paired = held.reshape(count, 2, span_rows, local_cols)
        side = layer_index >> level & 1
        keep_half = lax.dynamic_index_in_dim(paired, side, 1, keepdims=False)
        send_half = lax.dynamic_index_in_dim(paired, 1 - side, 1, keepdims=False)
        partner = from_partner(send_half, "layer", level)
        total = keep_half.astype(jnp.float32) + partner.astype(jnp.float32)
        stride = 2 ** (level + 1)
        base = layer_index % stride
        span_ids = base + stride * jnp.arange(count, dtype=jnp.int32)
        global_rows = (
            span_ids[:, None] * span_rows + jnp.arange(span_rows, dtype=jnp.int32)[None, :]
        ).reshape(count * span_rows)
        separator = sep_blocks[level]
        position = jnp.sum(jnp.where(col_order == separator, positions, 0))
        owner = position * NB // local_cols
        offset = position * NB - owner * local_cols
        sep_row = separator * NB
        sep_span = sep_row // span_rows
        inner = sep_row - sep_span * span_rows
        holds = sep_span % stride == base
        local_span = jnp.where(holds, sep_span // stride, 0)
        zero = jnp.zeros((), jnp.int32)
        rows_here = lax.dynamic_slice(
            total, (local_span, inner, zero), (1, NB, local_cols)
        ).reshape(NB, local_cols)
        masked = jnp.where(holds, rows_here, jnp.zeros_like(rows_here)).astype(jnp.bfloat16)
        upper_rows = share_rows(masked, level)
        flat = total.reshape(count * span_rows, local_cols)
        local_panel = lax.dynamic_slice_in_dim(flat, offset, NB, 1).astype(jnp.bfloat16)
        local_factor = jnp.dot(
            local_panel, pivot_inverse[level], preferred_element_type=jnp.float32
        ).astype(jnp.bfloat16)
        factor = broadcast(local_factor, "col", owner)
        updated = flat - jnp.dot(factor, upper_rows, preferred_element_type=jnp.float32)
        keep = (global_rows // NB != separator)[:, None] & (col_blocks != position)[None, :]
        kept = jnp.where(keep, updated, jnp.zeros_like(updated)).astype(jnp.bfloat16)
        held = kept.reshape(count, span_rows, local_cols)
    result = held.reshape(span_rows, local_cols)
    return result


def fits(mesh, args):
    layers, columns = mesh.shape["layer"], mesh.shape["col"]
    lower_panel, upper_panel, diag_inverse = args[:3]
    rows, width = lower_panel.shape[1] // columns, lower_panel.shape[2]
    cols = upper_panel.shape[2] // columns
    return (
        layers == 4
        and columns % layers == 0
        and rows % (2 * NB) == 0
        and cols % (2 * NB) == 0
        and width % (2 * NB) == 0
        and diag_inverse.shape[2] % NB == 0
    )


def solution(mesh):
    in_specs = (
        P("layer", "col", None),
        P("layer", None, "col"),
        P("layer", None, None, None),
        P(),
        P("layer", None, None),
        P(),
        P(),
    )
    out_specs = P("layer", "col")

    def run(*args):
        body = fused if fits(mesh, args) else shards
        return jax.shard_map(body, mesh=mesh, in_specs=in_specs, out_specs=out_specs, check_vma=False)(*args)

    return run
```

```python
import functools

import jax
import jax.numpy as jnp
from jax import lax
from jax.experimental import pallas as pl
from jax.experimental.pallas import tpu as pltpu
from jax.sharding import PartitionSpec as P

NB = 128
F32 = jnp.float32
BF16 = jnp.bfloat16
MESH = pl.DeviceIdType.MESH


def dot(a, b):
    return jnp.dot(a, b, preferred_element_type=F32)


def fused_kernel(
    col_count, l_ref, u_ref, d_ref, piv_ref, pat_ref, ord_ref, sep_ref, out_ref,
    lbuf, rbuf, pbuf, cin, xin, v0, vbase, vy, vr, vl, vsr, vsl, s_acc, s_own, s_core, s_tot, s_x,
    y_send, yb_send, yv_send, zr_send, zl_send, br_send, bl_send, vr_send, vl_send, l_recv, b_recv, vy_recv, vr_recv, vl_recv,
    c_send, c_recv, x_send, x_recv, s_send, s_recv,
):
    piece_rows, width = l_ref.shape
    half = piece_rows // 2
    cols = u_ref.shape[1]
    ext = rbuf.shape[1]
    nz = col_count // 2
    blocks = cols // NB
    per_half = half // NB
    few = max(piece_rows // 16, 16)
    layer = lax.axis_index("layer")
    core, xx = layer % 2, layer // 2
    ci = lax.axis_index("col")
    y, z = ci % 2, ci // 2
    core_peer = {"layer": layer + 1 - 2 * core}
    x_peer = {"layer": layer + 2 - 4 * xx}
    y_peer = {"col": ci + 1 - 2 * y}
    right, left = {"col": ci + 2}, {"col": ci - 2}
    has_right, has_left = z < nz - 1, z > 0
    first = ci * blocks

    def one_if(condition):
        return jnp.where(condition, 1.0, 0.0).astype(F32)

    def hot_row(k, block):
        return one_if(sep_ref[k] == block)

    def hot_col(k, b):
        return one_if(ord_ref[first + b] == sep_ref[k])


    def copy(src, dst, send, recv, peer):
        return pltpu.make_async_remote_copy(
            src_ref=src, dst_ref=dst, send_sem=send, recv_sem=recv, device_id=peer, device_id_type=MESH
        )

    def piece(p):
        return pl.ds(pl.multiple_of(p * piece_rows, piece_rows), piece_rows)

    def chunk(q):
        return pl.ds(pl.multiple_of(q * half, half), half)

    barrier = pltpu.get_barrier_semaphore()
    for peer in (core_peer, x_peer, y_peer):
        pl.semaphore_signal(barrier, inc=1, device_id=peer, device_id_type=MESH)

    @pl.when(has_right)
    def _():
        pl.semaphore_signal(barrier, inc=1, device_id=right, device_id_type=MESH)

    @pl.when(has_left)
    def _():
        pl.semaphore_signal(barrier, inc=1, device_id=left, device_id_type=MESH)

    for k in range(2):
        taken = u_ref[:, 0:NB].astype(F32) * hot_col(k, 0)
        for b in range(1, blocks):
            taken = taken + u_ref[:, b * NB : (b + 1) * NB].astype(F32) * hot_col(k, b)
        v0[:, k * NB : (k + 1) * NB] = taken.astype(BF16)

    pl.semaphore_wait(barrier, 3 + jnp.where(has_right, 1, 0) + jnp.where(has_left, 1, 0))

    parts = 4
    part = v0.shape[0] // parts
    y_first, z_first = (0, 1), (2, 3)

    def vpart(k):
        return pl.ds(k * part, part)

    def v_y(k):
        src = v0 if k in y_first else vbase
        return copy(src.at[vpart(k)], vy.at[vpart(k)], yv_send.at[k], vy_recv.at[k], y_peer)

    def v_right(k):
        return copy(vsr.at[vpart(k)], vr.at[vpart(k)], vr_send.at[k], vr_recv.at[k], right)

    def v_left(k):
        return copy(vsl.at[vpart(k)], vl.at[vpart(k)], vl_send.at[k], vl_recv.at[k], left)

    def add_right(k):
        rows = vpart(k)

        @pl.when(has_left)
        def _():
            v_right(k).wait_recv()
            vsr[rows, :] = vsr[rows, :] + vr[rows, :]

        @pl.when(has_right)
        def _():
            v_right(k).start()

    def add_left(k):
        rows = vpart(k)

        @pl.when(has_right)
        def _():
            v_left(k).wait_recv()
            vsl[rows, :] = vsl[rows, :] + vl[rows, :]

        @pl.when(has_left)
        def _():
            v_left(k).start()

    def near_way(k):
        pl.when(z < nz // 2)(functools.partial(add_right, k))
        pl.when(z >= nz // 2)(functools.partial(add_left, k))

    def far_way(k):
        pl.when(z < nz // 2)(functools.partial(add_left, k))
        pl.when(z >= nz // 2)(functools.partial(add_right, k))

    for k in y_first:
        v_y(k).start()
    vsr[...] = v0[...]
    vsl[...] = v0[...]

    @pl.when(z == 0)
    def _():
        for k in z_first:
            v_right(k).start()

    @pl.when(z == nz - 1)
    def _():
        for k in z_first:
            v_left(k).start()

    lbuf[piece(ci), :] = l_ref[...]

    def head(p, h):
        return pl.ds(pl.multiple_of(p * piece_rows + h * half, half), half - few * h)

    def tail(p):
        return pl.ds(pl.multiple_of(p * piece_rows + (piece_rows - few), few), few)

    def z_right(p, h):
        rows = chunk(2 * p + h)
        return copy(lbuf.at[rows], lbuf.at[rows], zr_send.at[p // 2 * 2 + h], l_recv.at[2 * p + h], right)

    def z_left(p, h):
        rows = chunk(2 * p + h)
        return copy(lbuf.at[rows], lbuf.at[rows], zl_send.at[p // 2 * 2 + h], l_recv.at[2 * p + h], left)

    def tail_right(p):
        return copy(lbuf.at[tail(p)], lbuf.at[tail(p)], br_send.at[p // 2], b_recv.at[p], right)

    def tail_left(p):
        return copy(lbuf.at[tail(p)], lbuf.at[tail(p)], bl_send.at[p // 2], b_recv.at[p], left)

    def over_y(p, h):
        rows = head(p, h)
        return copy(lbuf.at[rows], lbuf.at[rows], y_send.at[p // 2 * 2 + h], l_recv.at[2 * p + h], y_peer)

    def tail_over_y(p):
        return copy(lbuf.at[tail(p)], lbuf.at[tail(p)], yb_send.at[0], b_recv.at[p], y_peer)

    tail_over_y(ci).start()
    for h in range(2):
        over_y(ci, h).start()

        @pl.when(has_right)
        def _():
            z_right(ci, h).start()

        @pl.when(has_left)
        def _():
            z_left(ci, h).start()

    s_acc[...] = jnp.zeros_like(s_acc)

    @pl.when((z > 0) & (z < nz - 1))
    def _():
        for k in z_first:
            near_way(k)

    for k in y_first:
        rows = vpart(k)
        v_y(k).wait_recv()
        summed = v0[rows, :] + vy[rows, :]
        vbase[rows, :] = summed
        vsr[rows, :] = summed
        vsl[rows, :] = summed
        near_way(k)
    for k in z_first:
        rows = vpart(k)
        far_way(k)
        vbase[rows, :] = vsr[rows, :] + vsl[rows, :] - v0[rows, :]
        v_y(k).start()
    for k in y_first:
        far_way(k)

    other = ci + 1 - 2 * y
    tail_over_y(other).wait_recv()

    @pl.when(has_right)
    def _():
        tail_right(other).start()

    @pl.when(has_left)
    def _():
        tail_left(other).start()

    def pass_on(step):
        for h in range(2):
            for way in (1, -1):
                zc = z + way * (step + 1)

                @pl.when((zc >= 0) & (zc < nz))
                def _(zc=zc, way=way, h=h):
                    p, o = zc * 2 + y, zc * 2 + 1 - y
                    z_right(p, h).wait_recv()
                    on = has_left if way > 0 else has_right

                    @pl.when(on)
                    def _():
                        (z_left if way > 0 else z_right)(p, h).start()

                    over_y(p, h).start()
                    if h == 1:
                        tail_right(o).wait_recv()

                        @pl.when(on)
                        def _():
                            (tail_left if way > 0 else tail_right)(o).start()

    pass_on(0)

    supers, node = d_ref.shape[0], d_ref.shape[1]
    for s in range(supers):
        solved = dot(d_ref[s], u_ref[s * node : (s + 1) * node, :])
        rounded = solved.astype(BF16).astype(F32)
        for b in range(blocks):
            flag = -pat_ref[1, first + b].astype(F32)
            rbuf[s * node : (s + 1) * node, b * NB : (b + 1) * NB] = (
                rounded[:, b * NB : (b + 1) * NB] * flag
            ).astype(BF16)

    for k in z_first:
        rows = vpart(k)
        v_y(k).wait_recv()
        v0[rows, :] = vbase[rows, :] + vy[rows, :]
    for k in y_first:
        rows = vpart(k)
        v_y(k).wait_send()
        v0[rows, :] = vsr[rows, :] + vsl[rows, :] - vbase[rows, :]
    for s in range(supers):
        solved = dot(d_ref[s], v0[s * node : (s + 1) * node, :])
        rounded = solved.astype(BF16).astype(F32)
        for k in range(2):
            held = jnp.int32(0)
            for p in range(ord_ref.shape[0]):
                held = held + jnp.where(ord_ref[p] == sep_ref[k], pat_ref[1, p], 0)
            rbuf[s * node : (s + 1) * node, cols + k * NB : cols + (k + 1) * NB] = (
                rounded[:, k * NB : (k + 1) * NB] * -held.astype(F32)
            ).astype(BF16)

    per_span = col_count // 4

    span_halves = 2 * per_span

    def slot_of(q):
        return q // span_halves // 2 * span_halves + q % span_halves

    def to_core(q):
        slot = slot_of(q)
        return copy(pbuf.at[chunk(q)], cin.at[slot], c_send.at[slot], c_recv.at[slot], core_peer)

    def to_x(q):
        slot = q % span_halves
        return copy(pbuf.at[chunk(q)], xin.at[slot], x_send.at[slot], x_recv.at[slot], x_peer)

    def process(q):
        rows = lbuf[chunk(q), :]
        for n in range(0, ext, 2 * NB):
            acc = dot(rows, rbuf[:, n : n + 2 * NB])
            found = [None, None]
            for j in range(per_half):
                block = q * per_half + j
                flagged = acc[j * NB : (j + 1) * NB] * pat_ref[0, block].astype(F32)
                pbuf[pl.ds(pl.multiple_of(block * NB, NB), NB), n : n + 2 * NB] = flagged.astype(BF16)
                for k in range(2):
                    term = flagged * hot_row(k, block)
                    found[k] = term if j == 0 else found[k] + term
            for k in range(2):
                s_acc[k * NB : (k + 1) * NB, n : n + 2 * NB] += found[k]
        span = q // span_halves

        @pl.when(span % 2 != core)
        def _():
            to_core(q).start()

    def finish(q):
        span = q // span_halves

        @pl.when(span % 2 == core)
        def _():
            to_core(q).wait_recv()
            slot = slot_of(q)

            @pl.loop(0, per_half)
            def _(j):
                at = pl.ds(pl.multiple_of(q * half + j * NB, NB), NB)
                here = pl.ds(pl.multiple_of(j * NB, NB), NB)
                pbuf[at, :] = (pbuf[at, :].astype(F32) + cin[slot, here, :].astype(F32)).astype(BF16)

            @pl.when(span // 2 != xx)
            def _():
                to_x(q).start()

    def handle(step, line, arriving):
        def candidate(t):
            zc = z + step * (1 - 2 * (t % 2))
            valid = (zc >= 0) & (zc < nz) & ((step > 0) | (t % 2 == 0))
            return zc * 2 + line, t // 2, valid

        @pl.loop(0, 6)
        def _(t):
            p, h, valid = candidate(t)

            @pl.when((t < 4) & valid)
            def _():
                if arriving:

                    @pl.when(h == 0)
                    def _():
                        over_y(p, 0).wait_recv()

                    @pl.when(h == 1)
                    def _():
                        over_y(p, 1).wait_recv()

                process(2 * p + h)

            p_before, h_before, valid_before = candidate(jnp.maximum(t - 2, 0))

            @pl.when((t >= 2) & valid_before)
            def _():
                finish(2 * p_before + h_before)

    @pl.loop(0, nz)
    def _(step):
        handle(step, y, False)

        @pl.when(step > 0)
        def _():
            pass_on(step)

        handle(step, 1 - y, True)

    def s_copy(src, dst, k, peer):
        return copy(src, dst, s_send.at[k], s_recv.at[k], peer)

    s_own[...] = s_acc[...].astype(BF16)
    swap = s_copy(s_own, s_core, 0, core_peer)
    swap.start()
    swap.wait()
    s_tot[...] = (s_own[...].astype(F32) + s_core[...].astype(F32)).astype(BF16)
    mine = pl.ds(pl.multiple_of(core * NB, NB), NB)
    over_x = s_copy(s_tot.at[mine], s_x.at[mine], 1, x_peer)
    over_x.start()
    over_x.wait_recv()
    share = s_copy(s_x.at[mine], s_x.at[mine], 2, core_peer)
    share.start()
    share.wait_recv()

    pos_col = [cols, cols + NB]
    upper = jnp.concatenate([s_tot[0:NB, 0:cols], s_x[0:NB, 0:cols]], axis=0)
    upper_p = jnp.concatenate([s_tot[0:NB, pos_col[1] : ext], s_x[0:NB, pos_col[1] : ext]], axis=0)
    keep_c = [
        jnp.concatenate([jnp.full((1, NB), 1.0, F32) * (1.0 - hot_col(k, b)) for b in range(blocks)], axis=1)
        for k in range(2)
    ]

    def factors(a, b):
        return jnp.concatenate([dot(a, piv_ref[0]).astype(BF16), dot(b, piv_ref[0]).astype(BF16)], axis=1)

    fs = factors(s_tot[NB : 2 * NB, cols : cols + NB], s_x[NB : 2 * NB, cols : cols + NB])
    last = s_tot[NB : 2 * NB, 0:cols].astype(F32) + s_x[NB : 2 * NB, 0:cols].astype(F32)
    upper2 = ((last - dot(fs, upper)) * keep_c[0]).astype(BF16)

    for slot in range(span_halves):
        q = layer * span_halves + slot

        to_x(q).wait_recv()
        at = chunk(q)
        f0 = factors(pbuf[at, cols : cols + NB], xin[slot, :, cols : cols + NB])

        def keep_rows(value, k):
            kept = [
                value[j * NB : (j + 1) * NB] * (1.0 - hot_row(k, q * per_half + j)) for j in range(per_half)
            ]
            return jnp.concatenate(kept, axis=0)

        panel = pbuf[at, pos_col[1] : ext].astype(F32) + xin[slot, :, pos_col[1] : ext].astype(F32)
        panel = keep_rows(panel - dot(f0, upper_p), 0).astype(BF16)
        f2 = dot(panel, piv_ref[1]).astype(BF16)
        total = pbuf[at, 0:cols].astype(F32) + xin[slot, :, 0:cols].astype(F32)
        total = keep_rows(total - dot(f0, upper), 0) * keep_c[0]
        final = keep_rows(total - dot(f2, upper2), 1) * keep_c[1]
        out_ref[slot * half : (slot + 1) * half, :] = final.astype(BF16)

    over_x.wait_send()
    share.wait_send()
    for k in range(parts):
        if k in z_first:
            v_y(k).wait_send()

        @pl.when(has_right)
        def _():
            v_right(k).wait_send()

        @pl.when(has_left)
        def _():
            v_left(k).wait_send()

    tail_over_y(ci).wait_send()

    @pl.loop(0, nz)
    def _(zc):
        p, o = zc * 2 + y, zc * 2 + 1 - y
        for h in range(2):
            over_y(p, h).wait_send()

            @pl.when(has_right & (zc <= z))
            def _():
                z_right(p, h).wait_send()

            @pl.when(has_left & (zc >= z))
            def _():
                z_left(p, h).wait_send()

        @pl.when(has_right & (zc <= z))
        def _():
            tail_right(o).wait_send()

        @pl.when(has_left & (zc >= z))
        def _():
            tail_left(o).wait_send()

    @pl.loop(0, 2 * col_count)
    def _(q):
        span = q // span_halves

        @pl.when(span % 2 != core)
        def _():
            to_core(q).wait_send()

        @pl.when((span % 2 == core) & (span // 2 != xx))
        def _():
            to_x(q).wait_send()


def fused(lower_panel, upper_panel, diag_inverse, pivot_inverse, pattern, col_order, sep_blocks):
    col_count = lax.axis_size("col")
    piece_rows, width = lower_panel.shape[1:]
    cols = upper_panel.shape[2]
    ext = cols + 2 * NB
    nz, slots, half = col_count // 2, col_count, piece_rows // 2
    total_rows = piece_rows * col_count
    per_span = col_count // 4
    parts = 4
    vmem = pl.BlockSpec(memory_space=pltpu.VMEM)
    smem = pl.BlockSpec(memory_space=pltpu.SMEM)
    dma = pltpu.SemaphoreType.DMA
    v_shape = pltpu.VMEM((width, 2 * NB), BF16)
    s_shape = pltpu.VMEM((2 * NB, ext), BF16)
    return pl.pallas_call(
        functools.partial(fused_kernel, col_count),
        out_shape=jax.ShapeDtypeStruct((per_span * piece_rows, cols), BF16),
        in_specs=[vmem] * 4 + [smem] * 3,
        out_specs=vmem,
        scratch_shapes=[
            pltpu.VMEM((total_rows, width), BF16),
            pltpu.VMEM((width, ext), BF16),
            pltpu.VMEM((total_rows, ext), BF16),
            pltpu.VMEM((slots, half, ext), BF16),
            pltpu.VMEM((2 * per_span, half, ext), BF16),
            v_shape, v_shape, v_shape, v_shape, v_shape, v_shape, v_shape,
            pltpu.VMEM((2 * NB, ext), F32), s_shape, s_shape, s_shape, s_shape,
            dma((2 * nz,)), dma((1,)), dma((parts,)), dma((2 * nz,)), dma((2 * nz,)), dma((nz,)), dma((nz,)), dma((parts,)), dma((parts,)),
            dma((2 * col_count,)), dma((col_count,)), dma((parts,)), dma((parts,)), dma((parts,)),
            dma((slots,)), dma((slots,)), dma((2 * per_span,)), dma((2 * per_span,)), dma((3,)), dma((3,)),
        ],
        compiler_params=pltpu.CompilerParams(
            collective_id=0, has_side_effects=True, vmem_limit_bytes=56 * 2**20
        ),
        cost_estimate=pl.CostEstimate(flops=6 * 10**9, bytes_accessed=5 * 10**6, transcendentals=0),
    )(
        lower_panel[0], upper_panel[0], diag_inverse[0], pivot_inverse, pattern[0], col_order,
        sep_blocks,
    )


def from_partner(value, axis, distance):
    mask = 2**distance
    pairs = [(source, source ^ mask) for source in range(lax.axis_size(axis))]
    return lax.ppermute(value, axis, pairs)


def broadcast(x, axis, root):
    mine = lax.axis_index(axis) == root
    return lax.psum(jnp.where(mine, x, jnp.zeros_like(x)), axis)


def share_rows(values, level):
    for bit in range(level + 1):
        other = from_partner(values, "layer", bit)
        values = (values.astype(jnp.float32) + other.astype(jnp.float32)).astype(jnp.bfloat16)
    return values


def shards(lower_panel, upper_panel, diag_inverse, pivot_inverse, pattern, col_order, sep_blocks):
    supernodes = diag_inverse.shape[1]
    node_width = diag_inverse.shape[2]
    local_cols = upper_panel.shape[2]
    col_index = lax.axis_index("col")
    first_col = col_index * local_cols
    nblocks = col_order.shape[0]
    solved = jnp.einsum(
        "sab,sbc->sac",
        diag_inverse[0],
        upper_panel[0].reshape(supernodes, node_width, local_cols),
        preferred_element_type=jnp.float32,
    )
    right = solved.astype(jnp.bfloat16).reshape(supernodes * node_width, local_cols)
    row_flags = jnp.repeat(pattern[0, 0], NB).astype(jnp.float32)
    all_col_flags = jnp.repeat(pattern[0, 1], NB).astype(jnp.float32)
    col_flags = lax.dynamic_slice_in_dim(all_col_flags, first_col, local_cols)
    product = jnp.dot(
        lax.all_gather(lower_panel[0], "col", axis=0, tiled=True),
        right,
        preferred_element_type=jnp.float32,
    )
    current = (-product * row_flags[:, None] * col_flags[None, :]).astype(jnp.bfloat16)
    layer_count = lax.axis_size("layer")
    layer_index = lax.axis_index("layer")
    levels = layer_count.bit_length() - 1
    positions = jnp.arange(nblocks, dtype=jnp.int32)
    total_rows = current.shape[0]
    span_rows = total_rows // layer_count
    col_blocks = (first_col + jnp.arange(local_cols, dtype=jnp.int32)) // NB
    held = current.reshape(layer_count, span_rows, local_cols)
    for level in range(levels):
        count = held.shape[0] // 2
        paired = held.reshape(count, 2, span_rows, local_cols)
        side = layer_index >> level & 1
        keep_half = lax.dynamic_index_in_dim(paired, side, 1, keepdims=False)
        send_half = lax.dynamic_index_in_dim(paired, 1 - side, 1, keepdims=False)
        partner = from_partner(send_half, "layer", level)
        total = keep_half.astype(jnp.float32) + partner.astype(jnp.float32)
        stride = 2 ** (level + 1)
        base = layer_index % stride
        span_ids = base + stride * jnp.arange(count, dtype=jnp.int32)
        global_rows = (
            span_ids[:, None] * span_rows + jnp.arange(span_rows, dtype=jnp.int32)[None, :]
        ).reshape(count * span_rows)
        separator = sep_blocks[level]
        position = jnp.sum(jnp.where(col_order == separator, positions, 0))
        owner = position * NB // local_cols
        offset = position * NB - owner * local_cols
        sep_row = separator * NB
        sep_span = sep_row // span_rows
        inner = sep_row - sep_span * span_rows
        holds = sep_span % stride == base
        local_span = jnp.where(holds, sep_span // stride, 0)
        zero = jnp.zeros((), jnp.int32)
        rows_here = lax.dynamic_slice(
            total, (local_span, inner, zero), (1, NB, local_cols)
        ).reshape(NB, local_cols)
        masked = jnp.where(holds, rows_here, jnp.zeros_like(rows_here)).astype(jnp.bfloat16)
        upper_rows = share_rows(masked, level)
        flat = total.reshape(count * span_rows, local_cols)
        local_panel = lax.dynamic_slice_in_dim(flat, offset, NB, 1).astype(jnp.bfloat16)
        local_factor = jnp.dot(
            local_panel, pivot_inverse[level], preferred_element_type=jnp.float32
        ).astype(jnp.bfloat16)
        factor = broadcast(local_factor, "col", owner)
        updated = flat - jnp.dot(factor, upper_rows, preferred_element_type=jnp.float32)
        keep = (global_rows // NB != separator)[:, None] & (col_blocks != position)[None, :]
        kept = jnp.where(keep, updated, jnp.zeros_like(updated)).astype(jnp.bfloat16)
        held = kept.reshape(count, span_rows, local_cols)
    result = held.reshape(span_rows, local_cols)
    return result


def fits(mesh, args):
    layers, columns = mesh.shape["layer"], mesh.shape["col"]
    lower_panel, upper_panel, diag_inverse = args[:3]
    rows, width = lower_panel.shape[1] // columns, lower_panel.shape[2]
    cols = upper_panel.shape[2] // columns
    return (
        layers == 4
        and columns % layers == 0
        and rows % (2 * NB) == 0
        and cols % (2 * NB) == 0
        and width % (2 * NB) == 0
        and diag_inverse.shape[2] % NB == 0
    )


def solution(mesh):
    in_specs = (
        P("layer", "col", None),
        P("layer", None, "col"),
        P("layer", None, None, None),
        P(),
        P("layer", None, None),
        P(),
        P(),
    )
    out_specs = P("layer", "col")

    def run(*args):
        body = fused if fits(mesh, args) else shards
        return jax.shard_map(body, mesh=mesh, in_specs=in_specs, out_specs=out_specs, check_vma=False)(*args)

    return run
```

```python
import functools

import jax
import jax.numpy as jnp
from jax import lax
from jax.experimental import pallas as pl
from jax.experimental.pallas import tpu as pltpu
from jax.sharding import PartitionSpec as P

NB = 128
F32 = jnp.float32
BF16 = jnp.bfloat16
MESH = pl.DeviceIdType.MESH


def dot(a, b):
    return jnp.dot(a, b, preferred_element_type=F32)


def fused_kernel(
    col_count, l_ref, u_ref, d_ref, piv_ref, pat_ref, ord_ref, sep_ref, out_ref,
    lbuf, rbuf, pbuf, cin, xin, v0, vbase, vy, vr, vl, vsr, vsl, s_acc, s_own, s_core, s_tot, s_x,
    y_send, yb_send, yv_send, zr_send, zl_send, br_send, bl_send, vr_send, vl_send, l_recv, b_recv, vy_recv, vr_recv, vl_recv,
    c_send, c_recv, x_send, x_recv, s_send, s_recv,
):
    piece_rows, width = l_ref.shape
    half = piece_rows // 2
    cols = u_ref.shape[1]
    ext = rbuf.shape[1]
    nz = col_count // 2
    blocks = cols // NB
    per_half = half // NB
    few = max(piece_rows // 8, 16)
    layer = lax.axis_index("layer")
    core, xx = layer % 2, layer // 2
    ci = lax.axis_index("col")
    y, z = ci % 2, ci // 2
    core_peer = {"layer": layer + 1 - 2 * core}
    x_peer = {"layer": layer + 2 - 4 * xx}
    y_peer = {"col": ci + 1 - 2 * y}
    right, left = {"col": ci + 2}, {"col": ci - 2}
    has_right, has_left = z < nz - 1, z > 0
    first = ci * blocks

    def one_if(condition):
        return jnp.where(condition, 1.0, 0.0).astype(F32)

    def hot_row(k, block):
        return one_if(sep_ref[k] == block)

    def hot_col(k, b):
        return one_if(ord_ref[first + b] == sep_ref[k])


    def copy(src, dst, send, recv, peer):
        return pltpu.make_async_remote_copy(
            src_ref=src, dst_ref=dst, send_sem=send, recv_sem=recv, device_id=peer, device_id_type=MESH
        )

    def piece(p):
        return pl.ds(pl.multiple_of(p * piece_rows, piece_rows), piece_rows)

    def chunk(q):
        return pl.ds(pl.multiple_of(q * half, half), half)

    barrier = pltpu.get_barrier_semaphore()
    for peer in (core_peer, x_peer, y_peer):
        pl.semaphore_signal(barrier, inc=1, device_id=peer, device_id_type=MESH)

    @pl.when(has_right)
    def _():
        pl.semaphore_signal(barrier, inc=1, device_id=right, device_id_type=MESH)

    @pl.when(has_left)
    def _():
        pl.semaphore_signal(barrier, inc=1, device_id=left, device_id_type=MESH)

    for k in range(2):
        taken = u_ref[:, 0:NB].astype(F32) * hot_col(k, 0)
        for b in range(1, blocks):
            taken = taken + u_ref[:, b * NB : (b + 1) * NB].astype(F32) * hot_col(k, b)
        v0[:, k * NB : (k + 1) * NB] = taken.astype(BF16)

    pl.semaphore_wait(barrier, 3 + jnp.where(has_right, 1, 0) + jnp.where(has_left, 1, 0))

    parts = 4
    part = v0.shape[0] // parts
    y_first, z_first = (0, 1), (2, 3)

    def vpart(k):
        return pl.ds(k * part, part)

    def v_y(k):
        src = v0 if k in y_first else vbase
        return copy(src.at[vpart(k)], vy.at[vpart(k)], yv_send.at[k], vy_recv.at[k], y_peer)

    def v_right(k):
        return copy(vsr.at[vpart(k)], vr.at[vpart(k)], vr_send.at[k], vr_recv.at[k], right)

    def v_left(k):
        return copy(vsl.at[vpart(k)], vl.at[vpart(k)], vl_send.at[k], vl_recv.at[k], left)

    def add_right(k):
        rows = vpart(k)

        @pl.when(has_left)
        def _():
            v_right(k).wait_recv()
            vsr[rows, :] = vsr[rows, :] + vr[rows, :]

        @pl.when(has_right)
        def _():
            v_right(k).start()

    def add_left(k):
        rows = vpart(k)

        @pl.when(has_right)
        def _():
            v_left(k).wait_recv()
            vsl[rows, :] = vsl[rows, :] + vl[rows, :]

        @pl.when(has_left)
        def _():
            v_left(k).start()

    def near_way(k):
        pl.when(z < nz // 2)(functools.partial(add_right, k))
        pl.when(z >= nz // 2)(functools.partial(add_left, k))

    def far_way(k):
        pl.when(z < nz // 2)(functools.partial(add_left, k))
        pl.when(z >= nz // 2)(functools.partial(add_right, k))

    for k in y_first:
        v_y(k).start()
    vsr[...] = v0[...]
    vsl[...] = v0[...]

    @pl.when(z == 0)
    def _():
        for k in z_first:
            v_right(k).start()

    @pl.when(z == nz - 1)
    def _():
        for k in z_first:
            v_left(k).start()

    lbuf[piece(ci), :] = l_ref[...]

    def head(p, h):
        return pl.ds(pl.multiple_of(p * piece_rows + h * half, half), half - few * h)

    def tail(p):
        return pl.ds(pl.multiple_of(p * piece_rows + (piece_rows - few), few), few)

    def z_right(p, h):
        rows = chunk(2 * p + h)
        return copy(lbuf.at[rows], lbuf.at[rows], zr_send.at[p // 2 * 2 + h], l_recv.at[2 * p + h], right)

    def z_left(p, h):
        rows = chunk(2 * p + h)
        return copy(lbuf.at[rows], lbuf.at[rows], zl_send.at[p // 2 * 2 + h], l_recv.at[2 * p + h], left)

    def tail_right(p):
        return copy(lbuf.at[tail(p)], lbuf.at[tail(p)], br_send.at[p // 2], b_recv.at[p], right)

    def tail_left(p):
        return copy(lbuf.at[tail(p)], lbuf.at[tail(p)], bl_send.at[p // 2], b_recv.at[p], left)

    def over_y(p, h):
        rows = head(p, h)
        return copy(lbuf.at[rows], lbuf.at[rows], y_send.at[p // 2 * 2 + h], l_recv.at[2 * p + h], y_peer)

    def tail_over_y(p):
        return copy(lbuf.at[tail(p)], lbuf.at[tail(p)], yb_send.at[0], b_recv.at[p], y_peer)

    tail_over_y(ci).start()
    for h in range(2):
        over_y(ci, h).start()

        @pl.when(has_right)
        def _():
            z_right(ci, h).start()

        @pl.when(has_left)
        def _():
            z_left(ci, h).start()

    s_acc[...] = jnp.zeros_like(s_acc)

    @pl.when((z > 0) & (z < nz - 1))
    def _():
        for k in z_first:
            near_way(k)

    for k in y_first:
        rows = vpart(k)
        v_y(k).wait_recv()
        summed = v0[rows, :] + vy[rows, :]
        vbase[rows, :] = summed
        vsr[rows, :] = summed
        vsl[rows, :] = summed
        near_way(k)
    for k in z_first:
        rows = vpart(k)
        far_way(k)
        vbase[rows, :] = vsr[rows, :] + vsl[rows, :] - v0[rows, :]
        v_y(k).start()
    for k in y_first:
        far_way(k)

    other = ci + 1 - 2 * y
    tail_over_y(other).wait_recv()

    @pl.when(has_right)
    def _():
        tail_right(other).start()

    @pl.when(has_left)
    def _():
        tail_left(other).start()

    def pass_on(step):
        for h in range(2):
            for way in (1, -1):
                zc = z + way * (step + 1)

                @pl.when((zc >= 0) & (zc < nz))
                def _(zc=zc, way=way, h=h):
                    p, o = zc * 2 + y, zc * 2 + 1 - y
                    z_right(p, h).wait_recv()
                    on = has_left if way > 0 else has_right

                    @pl.when(on)
                    def _():
                        (z_left if way > 0 else z_right)(p, h).start()

                    over_y(p, h).start()
                    if h == 1:
                        tail_right(o).wait_recv()

                        @pl.when(on)
                        def _():
                            (tail_left if way > 0 else tail_right)(o).start()

    pass_on(0)

    supers, node = d_ref.shape[0], d_ref.shape[1]
    for s in range(supers):
        solved = dot(d_ref[s], u_ref[s * node : (s + 1) * node, :])
        rounded = solved.astype(BF16).astype(F32)
        for b in range(blocks):
            flag = -pat_ref[1, first + b].astype(F32)
            rbuf[s * node : (s + 1) * node, b * NB : (b + 1) * NB] = (
                rounded[:, b * NB : (b + 1) * NB] * flag
            ).astype(BF16)

    for k in z_first:
        rows = vpart(k)
        v_y(k).wait_recv()
        v0[rows, :] = vbase[rows, :] + vy[rows, :]
    for k in y_first:
        rows = vpart(k)
        v_y(k).wait_send()
        v0[rows, :] = vsr[rows, :] + vsl[rows, :] - vbase[rows, :]
    for s in range(supers):
        solved = dot(d_ref[s], v0[s * node : (s + 1) * node, :])
        rounded = solved.astype(BF16).astype(F32)
        for k in range(2):
            held = jnp.int32(0)
            for p in range(ord_ref.shape[0]):
                held = held + jnp.where(ord_ref[p] == sep_ref[k], pat_ref[1, p], 0)
            rbuf[s * node : (s + 1) * node, cols + k * NB : cols + (k + 1) * NB] = (
                rounded[:, k * NB : (k + 1) * NB] * -held.astype(F32)
            ).astype(BF16)

    per_span = col_count // 4

    span_halves = 2 * per_span

    def slot_of(q):
        return q // span_halves // 2 * span_halves + q % span_halves

    def to_core(q):
        slot = slot_of(q)
        return copy(pbuf.at[chunk(q)], cin.at[slot], c_send.at[slot], c_recv.at[slot], core_peer)

    def to_x(q):
        slot = q % span_halves
        return copy(pbuf.at[chunk(q)], xin.at[slot], x_send.at[slot], x_recv.at[slot], x_peer)

    def process(q):
        rows = lbuf[chunk(q), :]
        for n in range(0, ext, 2 * NB):
            acc = dot(rows, rbuf[:, n : n + 2 * NB])
            found = [None, None]
            for j in range(per_half):
                block = q * per_half + j
                flagged = acc[j * NB : (j + 1) * NB] * pat_ref[0, block].astype(F32)
                pbuf[pl.ds(pl.multiple_of(block * NB, NB), NB), n : n + 2 * NB] = flagged.astype(BF16)
                for k in range(2):
                    term = flagged * hot_row(k, block)
                    found[k] = term if j == 0 else found[k] + term
            for k in range(2):
                s_acc[k * NB : (k + 1) * NB, n : n + 2 * NB] += found[k]
        span = q // span_halves

        @pl.when(span % 2 != core)
        def _():
            to_core(q).start()

    def finish(q):
        span = q // span_halves

        @pl.when(span % 2 == core)
        def _():
            to_core(q).wait_recv()
            slot = slot_of(q)

            @pl.loop(0, per_half)
            def _(j):
                at = pl.ds(pl.multiple_of(q * half + j * NB, NB), NB)
                here = pl.ds(pl.multiple_of(j * NB, NB), NB)
                pbuf[at, :] = (pbuf[at, :].astype(F32) + cin[slot, here, :].astype(F32)).astype(BF16)

            @pl.when(span // 2 != xx)
            def _():
                to_x(q).start()

    def handle(step, line, arriving):
        def candidate(t):
            zc = z + step * (1 - 2 * (t % 2))
            valid = (zc >= 0) & (zc < nz) & ((step > 0) | (t % 2 == 0))
            return zc * 2 + line, t // 2, valid

        @pl.loop(0, 6)
        def _(t):
            p, h, valid = candidate(t)

            @pl.when((t < 4) & valid)
            def _():
                if arriving:

                    @pl.when(h == 0)
                    def _():
                        over_y(p, 0).wait_recv()

                    @pl.when(h == 1)
                    def _():
                        over_y(p, 1).wait_recv()

                process(2 * p + h)

            p_before, h_before, valid_before = candidate(jnp.maximum(t - 2, 0))

            @pl.when((t >= 2) & valid_before)
            def _():
                finish(2 * p_before + h_before)

    @pl.loop(0, nz)
    def _(step):
        handle(step, y, False)

        @pl.when(step > 0)
        def _():
            pass_on(step)

        handle(step, 1 - y, True)

    def s_copy(src, dst, k, peer):
        return copy(src, dst, s_send.at[k], s_recv.at[k], peer)

    s_own[...] = s_acc[...].astype(BF16)
    swap = s_copy(s_own, s_core, 0, core_peer)
    swap.start()
    swap.wait()
    s_tot[...] = (s_own[...].astype(F32) + s_core[...].astype(F32)).astype(BF16)
    mine = pl.ds(pl.multiple_of(core * NB, NB), NB)
    over_x = s_copy(s_tot.at[mine], s_x.at[mine], 1, x_peer)
    over_x.start()
    over_x.wait_recv()
    share = s_copy(s_x.at[mine], s_x.at[mine], 2, core_peer)
    share.start()
    share.wait_recv()

    pos_col = [cols, cols + NB]
    upper = jnp.concatenate([s_tot[0:NB, 0:cols], s_x[0:NB, 0:cols]], axis=0)
    upper_p = jnp.concatenate([s_tot[0:NB, pos_col[1] : ext], s_x[0:NB, pos_col[1] : ext]], axis=0)
    keep_c = [
        jnp.concatenate([jnp.full((1, NB), 1.0, F32) * (1.0 - hot_col(k, b)) for b in range(blocks)], axis=1)
        for k in range(2)
    ]

    def factors(a, b):
        return jnp.concatenate([dot(a, piv_ref[0]).astype(BF16), dot(b, piv_ref[0]).astype(BF16)], axis=1)

    fs = factors(s_tot[NB : 2 * NB, cols : cols + NB], s_x[NB : 2 * NB, cols : cols + NB])
    last = s_tot[NB : 2 * NB, 0:cols].astype(F32) + s_x[NB : 2 * NB, 0:cols].astype(F32)
    upper2 = ((last - dot(fs, upper)) * keep_c[0]).astype(BF16)

    for slot in range(span_halves):
        q = layer * span_halves + slot

        to_x(q).wait_recv()
        at = chunk(q)
        f0 = factors(pbuf[at, cols : cols + NB], xin[slot, :, cols : cols + NB])

        def keep_rows(value, k):
            kept = [
                value[j * NB : (j + 1) * NB] * (1.0 - hot_row(k, q * per_half + j)) for j in range(per_half)
            ]
            return jnp.concatenate(kept, axis=0)

        panel = pbuf[at, pos_col[1] : ext].astype(F32) + xin[slot, :, pos_col[1] : ext].astype(F32)
        panel = keep_rows(panel - dot(f0, upper_p), 0).astype(BF16)
        f2 = dot(panel, piv_ref[1]).astype(BF16)
        total = pbuf[at, 0:cols].astype(F32) + xin[slot, :, 0:cols].astype(F32)
        total = keep_rows(total - dot(f0, upper), 0) * keep_c[0]
        final = keep_rows(total - dot(f2, upper2), 1) * keep_c[1]
        out_ref[slot * half : (slot + 1) * half, :] = final.astype(BF16)

    over_x.wait_send()
    share.wait_send()
    for k in range(parts):
        if k in z_first:
            v_y(k).wait_send()

        @pl.when(has_right)
        def _():
            v_right(k).wait_send()

        @pl.when(has_left)
        def _():
            v_left(k).wait_send()

    tail_over_y(ci).wait_send()

    @pl.loop(0, nz)
    def _(zc):
        p, o = zc * 2 + y, zc * 2 + 1 - y
        for h in range(2):
            over_y(p, h).wait_send()

            @pl.when(has_right & (zc <= z))
            def _():
                z_right(p, h).wait_send()

            @pl.when(has_left & (zc >= z))
            def _():
                z_left(p, h).wait_send()

        @pl.when(has_right & (zc <= z))
        def _():
            tail_right(o).wait_send()

        @pl.when(has_left & (zc >= z))
        def _():
            tail_left(o).wait_send()

    @pl.loop(0, 2 * col_count)
    def _(q):
        span = q // span_halves

        @pl.when(span % 2 != core)
        def _():
            to_core(q).wait_send()

        @pl.when((span % 2 == core) & (span // 2 != xx))
        def _():
            to_x(q).wait_send()


def fused(lower_panel, upper_panel, diag_inverse, pivot_inverse, pattern, col_order, sep_blocks):
    col_count = lax.axis_size("col")
    piece_rows, width = lower_panel.shape[1:]
    cols = upper_panel.shape[2]
    ext = cols + 2 * NB
    nz, slots, half = col_count // 2, col_count, piece_rows // 2
    total_rows = piece_rows * col_count
    per_span = col_count // 4
    parts = 4
    vmem = pl.BlockSpec(memory_space=pltpu.VMEM)
    smem = pl.BlockSpec(memory_space=pltpu.SMEM)
    dma = pltpu.SemaphoreType.DMA
    v_shape = pltpu.VMEM((width, 2 * NB), BF16)
    s_shape = pltpu.VMEM((2 * NB, ext), BF16)
    return pl.pallas_call(
        functools.partial(fused_kernel, col_count),
        out_shape=jax.ShapeDtypeStruct((per_span * piece_rows, cols), BF16),
        in_specs=[vmem] * 4 + [smem] * 3,
        out_specs=vmem,
        scratch_shapes=[
            pltpu.VMEM((total_rows, width), BF16),
            pltpu.VMEM((width, ext), BF16),
            pltpu.VMEM((total_rows, ext), BF16),
            pltpu.VMEM((slots, half, ext), BF16),
            pltpu.VMEM((2 * per_span, half, ext), BF16),
            v_shape, v_shape, v_shape, v_shape, v_shape, v_shape, v_shape,
            pltpu.VMEM((2 * NB, ext), F32), s_shape, s_shape, s_shape, s_shape,
            dma((2 * nz,)), dma((1,)), dma((parts,)), dma((2 * nz,)), dma((2 * nz,)), dma((nz,)), dma((nz,)), dma((parts,)), dma((parts,)),
            dma((2 * col_count,)), dma((col_count,)), dma((parts,)), dma((parts,)), dma((parts,)),
            dma((slots,)), dma((slots,)), dma((2 * per_span,)), dma((2 * per_span,)), dma((3,)), dma((3,)),
        ],
        compiler_params=pltpu.CompilerParams(
            collective_id=0, has_side_effects=True, vmem_limit_bytes=56 * 2**20
        ),
        cost_estimate=pl.CostEstimate(flops=6 * 10**9, bytes_accessed=5 * 10**6, transcendentals=0),
    )(
        lower_panel[0], upper_panel[0], diag_inverse[0], pivot_inverse, pattern[0], col_order,
        sep_blocks,
    )


def from_partner(value, axis, distance):
    mask = 2**distance
    pairs = [(source, source ^ mask) for source in range(lax.axis_size(axis))]
    return lax.ppermute(value, axis, pairs)


def broadcast(x, axis, root):
    mine = lax.axis_index(axis) == root
    return lax.psum(jnp.where(mine, x, jnp.zeros_like(x)), axis)


def share_rows(values, level):
    for bit in range(level + 1):
        other = from_partner(values, "layer", bit)
        values = (values.astype(jnp.float32) + other.astype(jnp.float32)).astype(jnp.bfloat16)
    return values


def shards(lower_panel, upper_panel, diag_inverse, pivot_inverse, pattern, col_order, sep_blocks):
    supernodes = diag_inverse.shape[1]
    node_width = diag_inverse.shape[2]
    local_cols = upper_panel.shape[2]
    col_index = lax.axis_index("col")
    first_col = col_index * local_cols
    nblocks = col_order.shape[0]
    solved = jnp.einsum(
        "sab,sbc->sac",
        diag_inverse[0],
        upper_panel[0].reshape(supernodes, node_width, local_cols),
        preferred_element_type=jnp.float32,
    )
    right = solved.astype(jnp.bfloat16).reshape(supernodes * node_width, local_cols)
    row_flags = jnp.repeat(pattern[0, 0], NB).astype(jnp.float32)
    all_col_flags = jnp.repeat(pattern[0, 1], NB).astype(jnp.float32)
    col_flags = lax.dynamic_slice_in_dim(all_col_flags, first_col, local_cols)
    product = jnp.dot(
        lax.all_gather(lower_panel[0], "col", axis=0, tiled=True),
        right,
        preferred_element_type=jnp.float32,
    )
    current = (-product * row_flags[:, None] * col_flags[None, :]).astype(jnp.bfloat16)
    layer_count = lax.axis_size("layer")
    layer_index = lax.axis_index("layer")
    levels = layer_count.bit_length() - 1
    positions = jnp.arange(nblocks, dtype=jnp.int32)
    total_rows = current.shape[0]
    span_rows = total_rows // layer_count
    col_blocks = (first_col + jnp.arange(local_cols, dtype=jnp.int32)) // NB
    held = current.reshape(layer_count, span_rows, local_cols)
    for level in range(levels):
        count = held.shape[0] // 2
        paired = held.reshape(count, 2, span_rows, local_cols)
        side = layer_index >> level & 1
        keep_half = lax.dynamic_index_in_dim(paired, side, 1, keepdims=False)
        send_half = lax.dynamic_index_in_dim(paired, 1 - side, 1, keepdims=False)
        partner = from_partner(send_half, "layer", level)
        total = keep_half.astype(jnp.float32) + partner.astype(jnp.float32)
        stride = 2 ** (level + 1)
        base = layer_index % stride
        span_ids = base + stride * jnp.arange(count, dtype=jnp.int32)
        global_rows = (
            span_ids[:, None] * span_rows + jnp.arange(span_rows, dtype=jnp.int32)[None, :]
        ).reshape(count * span_rows)
        separator = sep_blocks[level]
        position = jnp.sum(jnp.where(col_order == separator, positions, 0))
        owner = position * NB // local_cols
        offset = position * NB - owner * local_cols
        sep_row = separator * NB
        sep_span = sep_row // span_rows
        inner = sep_row - sep_span * span_rows
        holds = sep_span % stride == base
        local_span = jnp.where(holds, sep_span // stride, 0)
        zero = jnp.zeros((), jnp.int32)
        rows_here = lax.dynamic_slice(
            total, (local_span, inner, zero), (1, NB, local_cols)
        ).reshape(NB, local_cols)
        masked = jnp.where(holds, rows_here, jnp.zeros_like(rows_here)).astype(jnp.bfloat16)
        upper_rows = share_rows(masked, level)
        flat = total.reshape(count * span_rows, local_cols)
        local_panel = lax.dynamic_slice_in_dim(flat, offset, NB, 1).astype(jnp.bfloat16)
        local_factor = jnp.dot(
            local_panel, pivot_inverse[level], preferred_element_type=jnp.float32
        ).astype(jnp.bfloat16)
        factor = broadcast(local_factor, "col", owner)
        updated = flat - jnp.dot(factor, upper_rows, preferred_element_type=jnp.float32)
        keep = (global_rows // NB != separator)[:, None] & (col_blocks != position)[None, :]
        kept = jnp.where(keep, updated, jnp.zeros_like(updated)).astype(jnp.bfloat16)
        held = kept.reshape(count, span_rows, local_cols)
    result = held.reshape(span_rows, local_cols)
    return result


def fits(mesh, args):
    layers, columns = mesh.shape["layer"], mesh.shape["col"]
    lower_panel, upper_panel, diag_inverse = args[:3]
    rows, width = lower_panel.shape[1] // columns, lower_panel.shape[2]
    cols = upper_panel.shape[2] // columns
    return (
        layers == 4
        and columns % layers == 0
        and rows % (2 * NB) == 0
        and cols % (2 * NB) == 0
        and width % (2 * NB) == 0
        and diag_inverse.shape[2] % NB == 0
    )


def solution(mesh):
    in_specs = (
        P("layer", "col", None),
        P("layer", None, "col"),
        P("layer", None, None, None),
        P(),
        P("layer", None, None),
        P(),
        P(),
    )
    out_specs = P("layer", "col")

    def run(*args):
        body = fused if fits(mesh, args) else shards
        return jax.shard_map(body, mesh=mesh, in_specs=in_specs, out_specs=out_specs, check_vma=False)(*args)

    return run
```

```python
import functools

import jax
import jax.numpy as jnp
from jax import lax
from jax.experimental import pallas as pl
from jax.experimental.pallas import tpu as pltpu
from jax.sharding import PartitionSpec as P

NB = 128
F32 = jnp.float32
BF16 = jnp.bfloat16
MESH = pl.DeviceIdType.MESH


def dot(a, b):
    return jnp.dot(a, b, preferred_element_type=F32)


def fused_kernel(
    col_count, l_ref, u_ref, d_ref, piv_ref, pat_ref, ord_ref, sep_ref, out_ref,
    lbuf, rbuf, pbuf, cin, xin, v0, vbase, vy, vr, vl, vsr, vsl, s_acc, s_own, s_core, s_tot, s_x,
    y_send, yb_send, yv_send, zr_send, zl_send, br_send, bl_send, vr_send, vl_send, l_recv, b_recv, vy_recv, vr_recv, vl_recv,
    c_send, c_recv, x_send, x_recv, s_send, s_recv,
):
    piece_rows, width = l_ref.shape
    half = piece_rows // 2
    cols = u_ref.shape[1]
    ext = rbuf.shape[1]
    nz = col_count // 2
    blocks = cols // NB
    per_half = half // NB
    few = max(piece_rows // 32, 16)
    layer = lax.axis_index("layer")
    core, xx = layer % 2, layer // 2
    ci = lax.axis_index("col")
    y, z = ci % 2, ci // 2
    core_peer = {"layer": layer + 1 - 2 * core}
    x_peer = {"layer": layer + 2 - 4 * xx}
    y_peer = {"col": ci + 1 - 2 * y}
    right, left = {"col": ci + 2}, {"col": ci - 2}
    has_right, has_left = z < nz - 1, z > 0
    first = ci * blocks

    def one_if(condition):
        return jnp.where(condition, 1.0, 0.0).astype(F32)

    def hot_row(k, block):
        return one_if(sep_ref[k] == block)

    def hot_col(k, b):
        return one_if(ord_ref[first + b] == sep_ref[k])


    def copy(src, dst, send, recv, peer):
        return pltpu.make_async_remote_copy(
            src_ref=src, dst_ref=dst, send_sem=send, recv_sem=recv, device_id=peer, device_id_type=MESH
        )

    def piece(p):
        return pl.ds(pl.multiple_of(p * piece_rows, piece_rows), piece_rows)

    def chunk(q):
        return pl.ds(pl.multiple_of(q * half, half), half)

    barrier = pltpu.get_barrier_semaphore()
    for peer in (core_peer, x_peer, y_peer):
        pl.semaphore_signal(barrier, inc=1, device_id=peer, device_id_type=MESH)

    @pl.when(has_right)
    def _():
        pl.semaphore_signal(barrier, inc=1, device_id=right, device_id_type=MESH)

    @pl.when(has_left)
    def _():
        pl.semaphore_signal(barrier, inc=1, device_id=left, device_id_type=MESH)

    for k in range(2):
        taken = u_ref[:, 0:NB].astype(F32) * hot_col(k, 0)
        for b in range(1, blocks):
            taken = taken + u_ref[:, b * NB : (b + 1) * NB].astype(F32) * hot_col(k, b)
        v0[:, k * NB : (k + 1) * NB] = taken.astype(BF16)

    pl.semaphore_wait(barrier, 3 + jnp.where(has_right, 1, 0) + jnp.where(has_left, 1, 0))

    parts = 2
    part = v0.shape[0] // (2 * parts)

    def vpart(k, line=y):
        return pl.ds(pl.multiple_of((line * parts + k) * part, part), part)

    def v_y(k):
        rows = vpart(k, 1 - y)
        return copy(v0.at[rows], vy.at[rows], yv_send.at[k], vy_recv.at[k], y_peer)

    def v_sum(k):
        rows = vpart(k)
        return copy(vbase.at[rows], vbase.at[rows], yv_send.at[parts + k], vy_recv.at[parts + k], y_peer)

    def v_right(k):
        return copy(vsr.at[vpart(k)], vr.at[vpart(k)], vr_send.at[k], vr_recv.at[k], right)

    def v_left(k):
        return copy(vsl.at[vpart(k)], vl.at[vpart(k)], vl_send.at[k], vl_recv.at[k], left)

    def add_right(k):
        rows = vpart(k)

        @pl.when(has_left)
        def _():
            v_right(k).wait_recv()
            vsr[rows, :] = vsr[rows, :] + vr[rows, :]

        @pl.when(has_right)
        def _():
            v_right(k).start()

    def add_left(k):
        rows = vpart(k)

        @pl.when(has_right)
        def _():
            v_left(k).wait_recv()
            vsl[rows, :] = vsl[rows, :] + vl[rows, :]

        @pl.when(has_left)
        def _():
            v_left(k).start()

    def near_way(k):
        pl.when(z < nz // 2)(functools.partial(add_right, k))
        pl.when(z >= nz // 2)(functools.partial(add_left, k))

    def far_way(k):
        pl.when(z < nz // 2)(functools.partial(add_left, k))
        pl.when(z >= nz // 2)(functools.partial(add_right, k))

    for k in range(parts):
        v_y(k).start()

    lbuf[piece(ci), :] = l_ref[...]

    def head(p, h):
        return pl.ds(pl.multiple_of(p * piece_rows + h * half, half), half - few * h)

    def tail(p):
        return pl.ds(pl.multiple_of(p * piece_rows + (piece_rows - few), few), few)

    def z_right(p, h):
        rows = chunk(2 * p + h)
        return copy(lbuf.at[rows], lbuf.at[rows], zr_send.at[p // 2 * 2 + h], l_recv.at[2 * p + h], right)

    def z_left(p, h):
        rows = chunk(2 * p + h)
        return copy(lbuf.at[rows], lbuf.at[rows], zl_send.at[p // 2 * 2 + h], l_recv.at[2 * p + h], left)

    def tail_right(p):
        return copy(lbuf.at[tail(p)], lbuf.at[tail(p)], br_send.at[p // 2], b_recv.at[p], right)

    def tail_left(p):
        return copy(lbuf.at[tail(p)], lbuf.at[tail(p)], bl_send.at[p // 2], b_recv.at[p], left)

    def over_y(p, h):
        rows = head(p, h)
        return copy(lbuf.at[rows], lbuf.at[rows], y_send.at[p // 2 * 2 + h], l_recv.at[2 * p + h], y_peer)

    def tail_over_y(p):
        return copy(lbuf.at[tail(p)], lbuf.at[tail(p)], yb_send.at[0], b_recv.at[p], y_peer)

    tail_over_y(ci).start()
    for h in range(2):
        over_y(ci, h).start()

        @pl.when(has_right)
        def _():
            z_right(ci, h).start()

        @pl.when(has_left)
        def _():
            z_left(ci, h).start()

    s_acc[...] = jnp.zeros_like(s_acc)

    for k in range(parts):
        rows = vpart(k)
        v_y(k).wait_recv()
        summed = v0[rows, :] + vy[rows, :]
        vbase[rows, :] = summed
        vsr[rows, :] = summed
        vsl[rows, :] = summed
        near_way(k)
    for k in range(parts):
        rows = vpart(k)
        far_way(k)
        vbase[rows, :] = vsr[rows, :] + vsl[rows, :] - vbase[rows, :]
        v_sum(k).start()

    other = ci + 1 - 2 * y
    tail_over_y(other).wait_recv()

    @pl.when(has_right)
    def _():
        tail_right(other).start()

    @pl.when(has_left)
    def _():
        tail_left(other).start()

    def pass_on(step):
        for h in range(2):
            for way in (1, -1):
                zc = z + way * (step + 1)

                @pl.when((zc >= 0) & (zc < nz))
                def _(zc=zc, way=way, h=h):
                    p, o = zc * 2 + y, zc * 2 + 1 - y
                    z_right(p, h).wait_recv()
                    on = has_left if way > 0 else has_right

                    @pl.when(on)
                    def _():
                        (z_left if way > 0 else z_right)(p, h).start()

                    over_y(p, h).start()
                    if h == 1:
                        tail_right(o).wait_recv()

                        @pl.when(on)
                        def _():
                            (tail_left if way > 0 else tail_right)(o).start()

    pass_on(0)

    supers, node = d_ref.shape[0], d_ref.shape[1]
    for s in range(supers):
        solved = dot(d_ref[s], u_ref[s * node : (s + 1) * node, :])
        rounded = solved.astype(BF16).astype(F32)
        for b in range(blocks):
            flag = -pat_ref[1, first + b].astype(F32)
            rbuf[s * node : (s + 1) * node, b * NB : (b + 1) * NB] = (
                rounded[:, b * NB : (b + 1) * NB] * flag
            ).astype(BF16)

    for k in range(parts):
        v_sum(k).wait_recv()
    for s in range(supers):
        solved = dot(d_ref[s], vbase[s * node : (s + 1) * node, :])
        rounded = solved.astype(BF16).astype(F32)
        for k in range(2):
            held = jnp.int32(0)
            for p in range(ord_ref.shape[0]):
                held = held + jnp.where(ord_ref[p] == sep_ref[k], pat_ref[1, p], 0)
            rbuf[s * node : (s + 1) * node, cols + k * NB : cols + (k + 1) * NB] = (
                rounded[:, k * NB : (k + 1) * NB] * -held.astype(F32)
            ).astype(BF16)

    per_span = col_count // 4

    span_halves = 2 * per_span

    def slot_of(q):
        return q // span_halves // 2 * span_halves + q % span_halves

    def to_core(q):
        slot = slot_of(q)
        return copy(pbuf.at[chunk(q)], cin.at[slot], c_send.at[slot], c_recv.at[slot], core_peer)

    def to_x(q):
        slot = q % span_halves
        return copy(pbuf.at[chunk(q)], xin.at[slot], x_send.at[slot], x_recv.at[slot], x_peer)

    def process(q):
        rows = lbuf[chunk(q), :]
        for n in range(0, ext, 2 * NB):
            acc = dot(rows, rbuf[:, n : n + 2 * NB])
            found = [None, None]
            for j in range(per_half):
                block = q * per_half + j
                flagged = acc[j * NB : (j + 1) * NB] * pat_ref[0, block].astype(F32)
                pbuf[pl.ds(pl.multiple_of(block * NB, NB), NB), n : n + 2 * NB] = flagged.astype(BF16)
                for k in range(2):
                    term = flagged * hot_row(k, block)
                    found[k] = term if j == 0 else found[k] + term
            for k in range(2):
                s_acc[k * NB : (k + 1) * NB, n : n + 2 * NB] += found[k]
        span = q // span_halves

        @pl.when(span % 2 != core)
        def _():
            to_core(q).start()

    def finish(q):
        span = q // span_halves

        @pl.when(span % 2 == core)
        def _():
            to_core(q).wait_recv()
            slot = slot_of(q)

            @pl.loop(0, per_half)
            def _(j):
                at = pl.ds(pl.multiple_of(q * half + j * NB, NB), NB)
                here = pl.ds(pl.multiple_of(j * NB, NB), NB)
                pbuf[at, :] = (pbuf[at, :].astype(F32) + cin[slot, here, :].astype(F32)).astype(BF16)

            @pl.when(span // 2 != xx)
            def _():
                to_x(q).start()

    def handle(step, line, arriving):
        def candidate(t):
            zc = z + step * (1 - 2 * (t % 2))
            valid = (zc >= 0) & (zc < nz) & ((step > 0) | (t % 2 == 0))
            return zc * 2 + line, t // 2, valid

        @pl.loop(0, 6)
        def _(t):
            p, h, valid = candidate(t)

            @pl.when((t < 4) & valid)
            def _():
                if arriving:

                    @pl.when(h == 0)
                    def _():
                        over_y(p, 0).wait_recv()

                    @pl.when(h == 1)
                    def _():
                        over_y(p, 1).wait_recv()

                process(2 * p + h)

            p_before, h_before, valid_before = candidate(jnp.maximum(t - 2, 0))

            @pl.when((t >= 2) & valid_before)
            def _():
                finish(2 * p_before + h_before)

    @pl.loop(0, nz)
    def _(step):
        handle(step, y, False)

        @pl.when(step > 0)
        def _():
            pass_on(step)

        handle(step, 1 - y, True)

    def s_copy(src, dst, k, peer):
        return copy(src, dst, s_send.at[k], s_recv.at[k], peer)

    s_own[...] = s_acc[...].astype(BF16)
    swap = s_copy(s_own, s_core, 0, core_peer)
    swap.start()
    swap.wait()
    s_tot[...] = (s_own[...].astype(F32) + s_core[...].astype(F32)).astype(BF16)
    mine = pl.ds(pl.multiple_of(core * NB, NB), NB)
    over_x = s_copy(s_tot.at[mine], s_x.at[mine], 1, x_peer)
    over_x.start()
    over_x.wait_recv()
    share = s_copy(s_x.at[mine], s_x.at[mine], 2, core_peer)
    share.start()
    share.wait_recv()

    pos_col = [cols, cols + NB]
    upper = jnp.concatenate([s_tot[0:NB, 0:cols], s_x[0:NB, 0:cols]], axis=0)
    upper_p = jnp.concatenate([s_tot[0:NB, pos_col[1] : ext], s_x[0:NB, pos_col[1] : ext]], axis=0)
    keep_c = [
        jnp.concatenate([jnp.full((1, NB), 1.0, F32) * (1.0 - hot_col(k, b)) for b in range(blocks)], axis=1)
        for k in range(2)
    ]

    def factors(a, b):
        return jnp.concatenate([dot(a, piv_ref[0]).astype(BF16), dot(b, piv_ref[0]).astype(BF16)], axis=1)

    fs = factors(s_tot[NB : 2 * NB, cols : cols + NB], s_x[NB : 2 * NB, cols : cols + NB])
    last = s_tot[NB : 2 * NB, 0:cols].astype(F32) + s_x[NB : 2 * NB, 0:cols].astype(F32)
    upper2 = ((last - dot(fs, upper)) * keep_c[0]).astype(BF16)

    for slot in range(span_halves):
        q = layer * span_halves + slot

        to_x(q).wait_recv()
        at = chunk(q)
        f0 = factors(pbuf[at, cols : cols + NB], xin[slot, :, cols : cols + NB])

        def keep_rows(value, k):
            kept = [
                value[j * NB : (j + 1) * NB] * (1.0 - hot_row(k, q * per_half + j)) for j in range(per_half)
            ]
            return jnp.concatenate(kept, axis=0)

        panel = pbuf[at, pos_col[1] : ext].astype(F32) + xin[slot, :, pos_col[1] : ext].astype(F32)
        panel = keep_rows(panel - dot(f0, upper_p), 0).astype(BF16)
        f2 = dot(panel, piv_ref[1]).astype(BF16)
        total = pbuf[at, 0:cols].astype(F32) + xin[slot, :, 0:cols].astype(F32)
        total = keep_rows(total - dot(f0, upper), 0) * keep_c[0]
        final = keep_rows(total - dot(f2, upper2), 1) * keep_c[1]
        out_ref[slot * half : (slot + 1) * half, :] = final.astype(BF16)

    over_x.wait_send()
    share.wait_send()
    for k in range(parts):
        v_y(k).wait_send()
        v_sum(k).wait_send()

        @pl.when(has_right)
        def _():
            v_right(k).wait_send()

        @pl.when(has_left)
        def _():
            v_left(k).wait_send()

    tail_over_y(ci).wait_send()

    @pl.loop(0, nz)
    def _(zc):
        p, o = zc * 2 + y, zc * 2 + 1 - y
        for h in range(2):
            over_y(p, h).wait_send()

            @pl.when(has_right & (zc <= z))
            def _():
                z_right(p, h).wait_send()

            @pl.when(has_left & (zc >= z))
            def _():
                z_left(p, h).wait_send()

        @pl.when(has_right & (zc <= z))
        def _():
            tail_right(o).wait_send()

        @pl.when(has_left & (zc >= z))
        def _():
            tail_left(o).wait_send()

    @pl.loop(0, 2 * col_count)
    def _(q):
        span = q // span_halves

        @pl.when(span % 2 != core)
        def _():
            to_core(q).wait_send()

        @pl.when((span % 2 == core) & (span // 2 != xx))
        def _():
            to_x(q).wait_send()


def fused(lower_panel, upper_panel, diag_inverse, pivot_inverse, pattern, col_order, sep_blocks):
    col_count = lax.axis_size("col")
    piece_rows, width = lower_panel.shape[1:]
    cols = upper_panel.shape[2]
    ext = cols + 2 * NB
    nz, slots, half = col_count // 2, col_count, piece_rows // 2
    total_rows = piece_rows * col_count
    per_span = col_count // 4
    parts = 4
    vmem = pl.BlockSpec(memory_space=pltpu.VMEM)
    smem = pl.BlockSpec(memory_space=pltpu.SMEM)
    dma = pltpu.SemaphoreType.DMA
    v_shape = pltpu.VMEM((width, 2 * NB), BF16)
    s_shape = pltpu.VMEM((2 * NB, ext), BF16)
    return pl.pallas_call(
        functools.partial(fused_kernel, col_count),
        out_shape=jax.ShapeDtypeStruct((per_span * piece_rows, cols), BF16),
        in_specs=[vmem] * 4 + [smem] * 3,
        out_specs=vmem,
        scratch_shapes=[
            pltpu.VMEM((total_rows, width), BF16),
            pltpu.VMEM((width, ext), BF16),
            pltpu.VMEM((total_rows, ext), BF16),
            pltpu.VMEM((slots, half, ext), BF16),
            pltpu.VMEM((2 * per_span, half, ext), BF16),
            v_shape, v_shape, v_shape, v_shape, v_shape, v_shape, v_shape,
            pltpu.VMEM((2 * NB, ext), F32), s_shape, s_shape, s_shape, s_shape,
            dma((2 * nz,)), dma((1,)), dma((parts,)), dma((2 * nz,)), dma((2 * nz,)), dma((nz,)), dma((nz,)), dma((parts,)), dma((parts,)),
            dma((2 * col_count,)), dma((col_count,)), dma((parts,)), dma((parts,)), dma((parts,)),
            dma((slots,)), dma((slots,)), dma((2 * per_span,)), dma((2 * per_span,)), dma((3,)), dma((3,)),
        ],
        compiler_params=pltpu.CompilerParams(
            collective_id=0, has_side_effects=True, vmem_limit_bytes=56 * 2**20
        ),
        cost_estimate=pl.CostEstimate(flops=6 * 10**9, bytes_accessed=5 * 10**6, transcendentals=0),
    )(
        lower_panel[0], upper_panel[0], diag_inverse[0], pivot_inverse, pattern[0], col_order,
        sep_blocks,
    )


def from_partner(value, axis, distance):
    mask = 2**distance
    pairs = [(source, source ^ mask) for source in range(lax.axis_size(axis))]
    return lax.ppermute(value, axis, pairs)


def broadcast(x, axis, root):
    mine = lax.axis_index(axis) == root
    return lax.psum(jnp.where(mine, x, jnp.zeros_like(x)), axis)


def share_rows(values, level):
    for bit in range(level + 1):
        other = from_partner(values, "layer", bit)
        values = (values.astype(jnp.float32) + other.astype(jnp.float32)).astype(jnp.bfloat16)
    return values


def shards(lower_panel, upper_panel, diag_inverse, pivot_inverse, pattern, col_order, sep_blocks):
    supernodes = diag_inverse.shape[1]
    node_width = diag_inverse.shape[2]
    local_cols = upper_panel.shape[2]
    col_index = lax.axis_index("col")
    first_col = col_index * local_cols
    nblocks = col_order.shape[0]
    solved = jnp.einsum(
        "sab,sbc->sac",
        diag_inverse[0],
        upper_panel[0].reshape(supernodes, node_width, local_cols),
        preferred_element_type=jnp.float32,
    )
    right = solved.astype(jnp.bfloat16).reshape(supernodes * node_width, local_cols)
    row_flags = jnp.repeat(pattern[0, 0], NB).astype(jnp.float32)
    all_col_flags = jnp.repeat(pattern[0, 1], NB).astype(jnp.float32)
    col_flags = lax.dynamic_slice_in_dim(all_col_flags, first_col, local_cols)
    product = jnp.dot(
        lax.all_gather(lower_panel[0], "col", axis=0, tiled=True),
        right,
        preferred_element_type=jnp.float32,
    )
    current = (-product * row_flags[:, None] * col_flags[None, :]).astype(jnp.bfloat16)
    layer_count = lax.axis_size("layer")
    layer_index = lax.axis_index("layer")
    levels = layer_count.bit_length() - 1
    positions = jnp.arange(nblocks, dtype=jnp.int32)
    total_rows = current.shape[0]
    span_rows = total_rows // layer_count
    col_blocks = (first_col + jnp.arange(local_cols, dtype=jnp.int32)) // NB
    held = current.reshape(layer_count, span_rows, local_cols)
    for level in range(levels):
        count = held.shape[0] // 2
        paired = held.reshape(count, 2, span_rows, local_cols)
        side = layer_index >> level & 1
        keep_half = lax.dynamic_index_in_dim(paired, side, 1, keepdims=False)
        send_half = lax.dynamic_index_in_dim(paired, 1 - side, 1, keepdims=False)
        partner = from_partner(send_half, "layer", level)
        total = keep_half.astype(jnp.float32) + partner.astype(jnp.float32)
        stride = 2 ** (level + 1)
        base = layer_index % stride
        span_ids = base + stride * jnp.arange(count, dtype=jnp.int32)
        global_rows = (
            span_ids[:, None] * span_rows + jnp.arange(span_rows, dtype=jnp.int32)[None, :]
        ).reshape(count * span_rows)
        separator = sep_blocks[level]
        position = jnp.sum(jnp.where(col_order == separator, positions, 0))
        owner = position * NB // local_cols
        offset = position * NB - owner * local_cols
        sep_row = separator * NB
        sep_span = sep_row // span_rows
        inner = sep_row - sep_span * span_rows
        holds = sep_span % stride == base
        local_span = jnp.where(holds, sep_span // stride, 0)
        zero = jnp.zeros((), jnp.int32)
        rows_here = lax.dynamic_slice(
            total, (local_span, inner, zero), (1, NB, local_cols)
        ).reshape(NB, local_cols)
        masked = jnp.where(holds, rows_here, jnp.zeros_like(rows_here)).astype(jnp.bfloat16)
        upper_rows = share_rows(masked, level)
        flat = total.reshape(count * span_rows, local_cols)
        local_panel = lax.dynamic_slice_in_dim(flat, offset, NB, 1).astype(jnp.bfloat16)
        local_factor = jnp.dot(
            local_panel, pivot_inverse[level], preferred_element_type=jnp.float32
        ).astype(jnp.bfloat16)
        factor = broadcast(local_factor, "col", owner)
        updated = flat - jnp.dot(factor, upper_rows, preferred_element_type=jnp.float32)
        keep = (global_rows // NB != separator)[:, None] & (col_blocks != position)[None, :]
        kept = jnp.where(keep, updated, jnp.zeros_like(updated)).astype(jnp.bfloat16)
        held = kept.reshape(count, span_rows, local_cols)
    result = held.reshape(span_rows, local_cols)
    return result


def fits(mesh, args):
    layers, columns = mesh.shape["layer"], mesh.shape["col"]
    lower_panel, upper_panel, diag_inverse = args[:3]
    rows, width = lower_panel.shape[1] // columns, lower_panel.shape[2]
    cols = upper_panel.shape[2] // columns
    return (
        layers == 4
        and columns % layers == 0
        and rows % (2 * NB) == 0
        and cols % (2 * NB) == 0
        and width % (2 * NB) == 0
        and diag_inverse.shape[2] % NB == 0
    )


def solution(mesh):
    in_specs = (
        P("layer", "col", None),
        P("layer", None, "col"),
        P("layer", None, None, None),
        P(),
        P("layer", None, None),
        P(),
        P(),
    )
    out_specs = P("layer", "col")

    def run(*args):
        body = fused if fits(mesh, args) else shards
        return jax.shard_map(body, mesh=mesh, in_specs=in_specs, out_specs=out_specs, check_vma=False)(*args)

    return run
```
